128 devices in a mesh: row: 8 (over z, x_hi), col: 8 (over y, core), ka: 2 (over x_lo).
Axes of the slice: x: 4 (x_hi: 2, x_lo: 2; x = x_hi * 2 + x_lo), y: 4, z: 4, core: 2. Of those that a mesh axis runs over, the one named last changes fastest.
Arguments:
- amplitudes: bfloat16 [4, 16, 1024, 1024], P(None, 'ka', 'row', 'col'), may hold values from -6 to 6
- integrals: bfloat16 [16, 1024, 4, 1024], P('ka', 'row', None, 'col'), may hold values from -0.046875 to 0.046875
Outputs:
- cycle_term: float32 [4, 4, 1024, 1024], P('ka', None, 'row', 'col')
The draws below stay inside these ranges and needn't reach their ends.
All inputs are finite; a program needn't handle non-finite values.
Results may differ from the reference program's by a relative error of at most 0.0003.
Values may be sent and summed in bfloat16 or wider, within the bound.
A program may use at most 64 MiB of HBM per device.

```python
import jax
import jax.numpy as jnp

NO = 4
V = 1024
KO = 16


def levels(stream_key, dims, shards, least, largest):
    def one(axis_at, blocks):
        heights = jax.random.uniform(jax.random.fold_in(jax.random.fold_in(stream_key, 6), axis_at), (blocks,), jnp.float32, least / len(shards), largest / len(shards))
        return jnp.repeat(jnp.exp(heights), dims[axis_at] // blocks).reshape((-1,) + (1,) * (len(dims) - axis_at - 1))

    gain = one(*shards[0])
    for cut in shards[1:]:
        gain = gain * one(*cut)
    return gain


def scatter_about(rng, dims, scale, bound, cuts=(), kind=jnp.bfloat16):
    factor_of = levels(rng, dims, cuts, -0.22, 0.18) if cuts else 1.0
    entries = jax.random.normal(rng, dims, jnp.float32) * scale * factor_of
    return jnp.minimum(jnp.maximum(entries, -bound), bound).astype(kind)


def setup_inputs(seed: int = 0) -> dict:
    key_of = jax.random.split(jax.random.key(seed), 3)
    return {
        "amplitudes": scatter_about(key_of[0], (NO, KO, V, V), 1.0, 6.0, ((1, 2), (2, 8), (3, 8))),
        "integrals": scatter_about(key_of[1], (KO, V, NO, V), (KO * V) ** -0.5, 0.046875, ((0, 2), (1, 8), (3, 8))),
    }


def reference(amplitudes, integrals):
    left = jnp.transpose(amplitudes, (0, 2, 1, 3)).reshape(NO * V, KO * V)
    right = integrals.reshape(KO * V, NO * V)
    cycle = jnp.dot(left, right, preferred_element_type=jnp.float32).reshape(NO, V, NO, V)
    return jnp.transpose(cycle, (0, 2, 1, 3)) + jnp.transpose(cycle, (2, 0, 3, 1))
```

```python
import jax
import jax.numpy as jnp
from jax import lax
from jax.experimental import pallas as pl
from jax.experimental.pallas import tpu as pltpu
from jax.sharding import PartitionSpec as P

MESH = pl.DeviceIdType.MESH
CHUNKS = 4
ROWS = 32
F32 = jnp.float32
BF16 = jnp.bfloat16


def phase_blocks(t):
    blocks = [(t, jj) for jj in range(t + 1)] + [(u, t) for u in range(t)]
    even = [b for b in blocks if b[1] % 2 == 0]
    return even, [b for b in blocks if b[1] % 2 == 1]


ORDER = [b for t in range(CHUNKS) for half in phase_blocks(t) for b in half]
PLACE = {b: e for e, b in enumerate(ORDER)}


def send(src, dst, send_sem, recv_sem, device):
    return pltpu.make_async_remote_copy(
        src_ref=src,
        dst_ref=dst,
        send_sem=send_sem,
        recv_sem=recv_sem,
        device_id=device,
        device_id_type=MESH,
    )


def arrived(ref, sem):
    pltpu.make_async_copy(ref, ref, sem).wait()


def kernel(
    a_in, b_in, out,
    a_all, b_all, b_raw, b_wide, part, sums, total, mirror,
    b_sem, a_ready, swap_send,
    an_send, an_recv, af_send, af_recv, as_send, as_recv,
    bn_send, bn_recv, bf_send, bf_recv,
    rs_send, rs_recv, t_send, t_recv,
):
    row, col, l = lax.axis_index("row"), lax.axis_index("col"), lax.axis_index("ka")
    z, h = row // 2, row % 2
    y, p = col // 2, col % 2
    x = 2 * h + l

    def dev(x, y, z, p):
        return (z * 2 + x // 2, y * 2 + p, x % 2)

    yp, ym, ya = (y + 1) % 4, (y + 3) % 4, (y + 2) % 4
    zp, zm, za = (z + 1) % 4, (z + 3) % 4, (z + 2) % 4
    y_next, y_prev = dev(x, yp, z, p), dev(x, ym, z, p)
    z_next, z_prev = dev(x, y, zp, p), dev(x, y, zm, p)
    sibling = dev(x, y, z, 1 - p)
    partner = dev((x + 2) % 4, y, z, 1 - p)
    x_others = [dev((x + d) % 4, y, z, p) for d in (1, 2, 3)]
    mirrors = [dev(2 * p + t, z, y, h) for t in (0, 1)]
    swaps = p != h
    on_self = jnp.logical_and(y == z, p == h)

    def j_of(jj):
        return ((jj % 2 + p) % 2) * 2 + jj // 2

    b_copy = pltpu.make_async_copy(b_in, b_raw, b_sem)
    b_copy.start()

    @pl.when(jnp.logical_not(swaps))
    def _():
        for u in range(CHUNKS):
            pltpu.make_async_copy(
                a_in.at[:, :, pl.ds(u * ROWS, ROWS), :], a_all.at[u, p, y], a_ready.at[u]
            ).start()

    barrier = pltpu.get_barrier_semaphore()

    def greet(device):
        pl.semaphore_signal(barrier, inc=1, device_id=device, device_id_type=MESH)

    for device in [y_next, y_prev, z_next, z_prev, sibling] + x_others:
        greet(device)

    @pl.when(swaps)
    def _():
        greet(partner)

    for t in (0, 1):
        @pl.when(jnp.logical_not(jnp.logical_and(on_self, l == t)))
        def _(t=t):
            greet(mirrors[t])

    b_copy.wait()
    for k in range(8):
        b_wide[k] = b_raw[k].astype(F32)
    for j in (0, 2, 1, 3):
        jj = (j % 2) * 2 + (j // 2 + p) % 2
        for k in range(8):
            b_all[jj, z, k] = b_wide[k, pl.ds(j, 128, stride=4), :].astype(BF16)

    peers = 9 + jnp.where(swaps, 1, 0) + jnp.where(on_self, 0, 1)
    pl.semaphore_wait(barrier, peers)

    def swap(u):
        return send(
            a_in.at[:, :, pl.ds(u * ROWS, ROWS), :],
            a_all.at[u, 1 - p, y],
            swap_send.at[u],
            a_ready.at[u],
            partner,
        )

    @pl.when(swaps)
    def _():
        for u in range(CHUNKS):
            swap(u).start()

    def a_near(u):
        slot = a_all.at[u, p, y]
        return [
            send(slot, slot, an_send.at[u, 0], an_recv.at[u, 0], y_next),
            send(slot, slot, an_send.at[u, 1], an_recv.at[u, 1], y_prev),
        ]

    def b_near(u):
        slot = b_all.at[u, z]
        return [
            send(slot, slot, bn_send.at[u, 0], bn_recv.at[u, 0], z_next),
            send(slot, slot, bn_send.at[u, 1], bn_recv.at[u, 1], z_prev),
        ]

    def a_far(u):
        one, two = a_all.at[u, p, ym, pl.ds(0, 2)], a_all.at[u, p, yp, pl.ds(2, 2)]
        return [
            send(one, one, af_send.at[u, 0], af_recv.at[u, 0], y_next),
            send(two, two, af_send.at[u, 1], af_recv.at[u, 1], y_prev),
        ]

    def b_far(u):
        one, two = b_all.at[u, zm, pl.ds(0, 4)], b_all.at[u, zp, pl.ds(4, 4)]
        return [
            send(one, one, bf_send.at[u, 0], bf_recv.at[u, 0], z_next),
            send(two, two, bf_send.at[u, 1], bf_recv.at[u, 1], z_prev),
        ]

    def a_side(u, n):
        slot = a_all.at[u, p, (y, ym, yp, ya)[n]]
        return send(slot, slot, as_send.at[u, n], as_recv.at[u, n], sibling)

    def own(u):
        arrived(a_all.at[u, p, y], a_ready.at[u])
        for copy in b_near(u) + a_near(u):
            copy.start()
        a_side(u, 0).start()

    def forward(u):
        b_copies, a_copies = b_far(u), a_far(u)
        arrived(b_all.at[u, zm], bn_recv.at[u, 0])
        b_copies[0].start()
        arrived(a_all.at[u, p, ym], an_recv.at[u, 0])
        a_copies[0].start()
        a_side(u, 1).start()
        arrived(b_all.at[u, zp], bn_recv.at[u, 1])
        b_copies[1].start()
        arrived(a_all.at[u, p, yp], an_recv.at[u, 1])
        a_copies[1].start()
        a_side(u, 2).start()

    def rs_copy(t, d):
        lo, size = t * t, 2 * t + 1
        there = (x + d) % 4
        return send(
            part.at[there // 2, pl.ds(lo, size), pl.ds((there % 2) * 2, 2)],
            sums.at[d - 1, pl.ds(lo, size)],
            rs_send.at[t, d - 1],
            rs_recv.at[t, d - 1],
            x_others[d - 1],
        )

    def multiply(t):
        arrived(a_all.at[t, p, ya, pl.ds(0, 2)], af_recv.at[t, 0])
        arrived(a_all.at[t, p, ya, pl.ds(2, 2)], af_recv.at[t, 1])
        a_side(t, 3).start()
        arrived(b_all.at[t, za, pl.ds(0, 4)], bf_recv.at[t, 0])
        arrived(b_all.at[t, za, pl.ds(4, 4)], bf_recv.at[t, 1])
        for n, place in enumerate((y, ym, yp, ya)):
            arrived(a_all.at[t, 1 - p, place], as_recv.at[t, n])
        for half in phase_blocks(t):
            for u, jj in half:
                def step(s, acc, u=u, jj=jj):
                    left = jnp.concatenate(
                        [a_all[u, :, s, :, k].reshape(8 * ROWS, 128) for k in range(8)], axis=1
                    )
                    right = b_all[jj, s].reshape(1024, 128)
                    return acc + jnp.dot(left, right, preferred_element_type=F32)

                acc = lax.fori_loop(0, 4, step, jnp.zeros((8 * ROWS, 128), F32))
                part[:, PLACE[u, jj]] = acc.reshape(2, 4, ROWS, 128)
        for d in (2, 1, 3):
            rs_copy(t, d).start()

    def span_of(t, half):
        even, odd = phase_blocks(t)
        return pl.ds(t * t + half * len(even), len(odd if half else even))

    def mirror_remote(t, half):
        span = span_of(t, half)
        there = dev(2 * p + (half + p) % 2, z, y, h)
        return send(total.at[span], mirror.at[l, span], t_send.at[t, half], t_recv.at[t, l], there)

    def mirror_local(t, half):
        span = span_of(t, half)
        return pltpu.make_async_copy(total.at[span], mirror.at[l, span], t_recv.at[t, l])

    def mirror_here(half):
        return jnp.logical_and(on_self, (half + p) % 2 == l)

    def reduce(t):
        lo, size = t * t, 2 * t + 1
        for d in (1, 3, 2):
            arrived(sums.at[d - 1, pl.ds(lo, size)], rs_recv.at[t, d - 1])
        for half in phase_blocks(t):
            for u, jj in half:
                e = PLACE[u, jj]
                value = part[h, e, pl.ds(2 * l, 2)] + sums[0, e] + sums[1, e] + sums[2, e]
                total[e] = value
                out[:, j_of(jj), pl.ds(u * ROWS, ROWS), :] = value
        for half in (0, 1):
            if phase_blocks(t)[half]:
                @pl.when(mirror_here(half))
                def _(half=half):
                    mirror_local(t, half).start()

                @pl.when(jnp.logical_not(mirror_here(half)))
                def _(half=half):
                    mirror_remote(t, half).start()

    own(0)
    own(1)
    for t in range(CHUNKS):
        forward(t)
        if t + 2 < CHUNKS:
            own(t + 2)
        if t >= 1:
            multiply(t - 1)
        if t >= 2:
            reduce(t - 2)
    multiply(CHUNKS - 1)
    reduce(CHUNKS - 2)
    reduce(CHUNKS - 1)

    for half in (0, 1):
        @pl.when((l + h) % 2 == half)
        def _(half=half):
            for t in range(CHUNKS):
                if phase_blocks(t)[half]:
                    for n in (0, 1):
                        arrived(mirror.at[n, span_of(t, half)], t_recv.at[t, n])
            for i in (0, 1):
                for n in (0, 1):
                    for m in (0, 1):
                        tile = jnp.concatenate(
                            [mirror[n, PLACE[u, 2 * i + half], m] for u in range(CHUNKS)], axis=0
                        )
                        out[i, 2 * n + m] = out[i, 2 * n + m] + tile.T

    for t in range(CHUNKS):
        for copy in a_near(t) + b_near(t) + a_far(t) + b_far(t):
            copy.wait_send()
        for n in range(4):
            a_side(t, n).wait_send()
        for d in (1, 2, 3):
            rs_copy(t, d).wait_send()
        for half in (0, 1):
            if phase_blocks(t)[half]:
                @pl.when(jnp.logical_not(mirror_here(half)))
                def _(t=t, half=half):
                    mirror_remote(t, half).wait_send()

    @pl.when(swaps)
    def _():
        for u in range(CHUNKS):
            swap(u).wait_send()


def per_device(amplitudes, integrals):
    rows = integrals.reshape(8, 512, 128)
    dma = pltpu.SemaphoreType.DMA
    n = CHUNKS
    return pl.pallas_call(
        kernel,
        out_shape=jax.ShapeDtypeStruct((2, 4, 128, 128), F32),
        in_specs=[pl.BlockSpec(memory_space=pl.ANY)] * 2,
        out_specs=pl.BlockSpec(memory_space=pltpu.VMEM),
        scratch_shapes=[
            pltpu.VMEM((n, 2, 4, 4, 8, ROWS, 128), BF16),
            pltpu.VMEM((4, 4, 8, 128, 128), BF16),
            pltpu.VMEM((8, 512, 128), BF16),
            pltpu.VMEM((8, 512, 128), F32),
            pltpu.VMEM((2, n * n, 4, ROWS, 128), F32),
            pltpu.VMEM((3, n * n, 2, ROWS, 128), F32),
            pltpu.VMEM((n * n, 2, ROWS, 128), F32),
            pltpu.VMEM((2, n * n, 2, ROWS, 128), F32),
            dma, dma((n,)), dma((n,)),
            dma((n, 2)), dma((n, 2)), dma((n, 2)), dma((n, 2)), dma((n, 4)), dma((n, 4)),
            dma((n, 2)), dma((n, 2)), dma((n, 2)), dma((n, 2)),
            dma((n, 3)), dma((n, 3)), dma((n, 2)), dma((n, 2)),
        ],
        compiler_params=pltpu.CompilerParams(
            collective_id=0, has_side_effects=True, vmem_limit_bytes=48 << 20
        ),
        cost_estimate=pl.CostEstimate(flops=4 << 30, bytes_accessed=3 << 20, transcendentals=0),
        name="cycle_contraction",
    )(amplitudes, rows)


def solution(mesh):
    return jax.shard_map(
        per_device,
        mesh=mesh,
        in_specs=(P(None, "ka", "row", "col"), P("ka", "row", None, "col")),
        out_specs=P("ka", None, "row", "col"),
        check_vma=False,
    )
```

```python
import jax
import jax.numpy as jnp
from jax import lax
from jax.experimental import pallas as pl
from jax.experimental.pallas import tpu as pltpu
from jax.sharding import PartitionSpec as P

MESH = pl.DeviceIdType.MESH
CHUNKS = 4
ROWS = 32
F32 = jnp.float32
BF16 = jnp.bfloat16


GROUPS = [
    [((t,), (jj, jj + 1)[: t + 1 - jj]) for jj in range(0, t + 1, 2)] + ([(tuple(range(t)), (t,))] if t else [])
    for t in range(CHUNKS)
]
FLAT = [(t, group) for t in range(CHUNKS) for group in GROUPS[t]]
PLACE = {}
FIRST = []
for _, (us, jjs) in FLAT:
    FIRST.append(len(PLACE))
    for jj in jjs:
        for u in us:
            PLACE[u, jj] = len(PLACE)
RUNS = [
    (g, PLACE[us[0], jj], len(us), jj % 2)
    for g, (_, (us, jjs)) in enumerate(FLAT)
    for jj in jjs
]


def send(src, dst, send_sem, recv_sem, device):
    return pltpu.make_async_remote_copy(
        src_ref=src,
        dst_ref=dst,
        send_sem=send_sem,
        recv_sem=recv_sem,
        device_id=device,
        device_id_type=MESH,
    )


def arrived(ref, sem):
    pltpu.make_async_copy(ref, ref, sem).wait()


def kernel(
    a_in, b_in, out,
    a_all, b_all, b_raw, b_wide, part, sums, total, mirror,
    b_sem, a_ready, swap_send,
    an_send, an_recv, af_send, af_recv, as_send, as_recv,
    bn_send, bn_recv, bf_send, bf_recv,
    rs_send, rs_recv, t_send, t_recv,
):
    row, col, l = lax.axis_index("row"), lax.axis_index("col"), lax.axis_index("ka")
    z, h = row // 2, row % 2
    y, p = col // 2, col % 2
    x = 2 * h + l

    def dev(x, y, z, p):
        return (z * 2 + x // 2, y * 2 + p, x % 2)

    yp, ym, ya = (y + 1) % 4, (y + 3) % 4, (y + 2) % 4
    zp, zm, za = (z + 1) % 4, (z + 3) % 4, (z + 2) % 4
    y_next, y_prev = dev(x, yp, z, p), dev(x, ym, z, p)
    z_next, z_prev = dev(x, y, zp, p), dev(x, y, zm, p)
    sibling = dev(x, y, z, 1 - p)
    partner = dev((x + 2) % 4, y, z, 1 - p)
    x_others = [dev((x + d) % 4, y, z, p) for d in (1, 2, 3)]
    mirrors = [dev(2 * p + t, z, y, h) for t in (0, 1)]
    swaps = p != h
    on_self = jnp.logical_and(y == z, p == h)

    def j_of(jj):
        return ((jj % 2 + p) % 2) * 2 + jj // 2

    b_copy = pltpu.make_async_copy(b_in, b_raw, b_sem)
    b_copy.start()

    @pl.when(jnp.logical_not(swaps))
    def _():
        for u in range(CHUNKS):
            pltpu.make_async_copy(
                a_in.at[:, :, pl.ds(u * ROWS, ROWS), :], a_all.at[u, p, y], a_ready.at[u]
            ).start()

    barrier = pltpu.get_barrier_semaphore()

    def greet(device):
        pl.semaphore_signal(barrier, inc=1, device_id=device, device_id_type=MESH)

    for device in [y_next, y_prev, z_next, z_prev, sibling] + x_others:
        greet(device)

    @pl.when(swaps)
    def _():
        greet(partner)

    for t in (0, 1):
        @pl.when(jnp.logical_not(jnp.logical_and(on_self, l == t)))
        def _(t=t):
            greet(mirrors[t])

    b_copy.wait()
    for k in range(8):
        b_wide[k] = b_raw[k].astype(F32)
    for j in (0, 2, 1, 3):
        jj = (j % 2) * 2 + (j // 2 + p) % 2
        for k in range(8):
            b_all[jj, z, k] = b_wide[k, pl.ds(j, 128, stride=4), :].astype(BF16)

    peers = 9 + jnp.where(swaps, 1, 0) + jnp.where(on_self, 0, 1)
    pl.semaphore_wait(barrier, peers)

    def swap(u):
        return send(
            a_in.at[:, :, pl.ds(u * ROWS, ROWS), :],
            a_all.at[u, 1 - p, y],
            swap_send.at[u],
            a_ready.at[u],
            partner,
        )

    def start_swap(u):
        @pl.when(swaps)
        def _():
            swap(u).start()

    start_swap(0)
    start_swap(1)

    def a_near(u):
        slot = a_all.at[u, p, y]
        return [
            send(slot, slot, an_send.at[u, 0], an_recv.at[u, 0], y_next),
            send(slot, slot, an_send.at[u, 1], an_recv.at[u, 1], y_prev),
        ]

    def b_near(u):
        slot = b_all.at[u, z]
        return [
            send(slot, slot, bn_send.at[u, 0], bn_recv.at[u, 0], z_next),
            send(slot, slot, bn_send.at[u, 1], bn_recv.at[u, 1], z_prev),
        ]

    def a_far(u):
        one, two = a_all.at[u, p, ym, pl.ds(0, 2)], a_all.at[u, p, yp, pl.ds(2, 2)]
        return [
            send(one, one, af_send.at[u, 0], af_recv.at[u, 0], y_next),
            send(two, two, af_send.at[u, 1], af_recv.at[u, 1], y_prev),
        ]

    def b_far(u):
        one, two = b_all.at[u, zm, pl.ds(0, 4)], b_all.at[u, zp, pl.ds(4, 4)]
        return [
            send(one, one, bf_send.at[u, 0], bf_recv.at[u, 0], z_next),
            send(two, two, bf_send.at[u, 1], bf_recv.at[u, 1], z_prev),
        ]

    def a_side(u, n):
        slot = a_all.at[u, p, (y, ym, yp, ya)[n]]
        return send(slot, slot, as_send.at[u, n], as_recv.at[u, n], sibling)

    def own(u):
        arrived(a_all.at[u, p, y], a_ready.at[u])
        if u + 2 < CHUNKS:
            start_swap(u + 2)
        for copy in b_near(u) + a_near(u):
            copy.start()
        a_side(u, 0).start()

    def forward(u):
        b_copies, a_copies = b_far(u), a_far(u)
        arrived(b_all.at[u, zm], bn_recv.at[u, 0])
        b_copies[0].start()
        arrived(a_all.at[u, p, ym], an_recv.at[u, 0])
        a_copies[0].start()
        a_side(u, 1).start()
        arrived(b_all.at[u, zp], bn_recv.at[u, 1])
        b_copies[1].start()
        arrived(a_all.at[u, p, yp], an_recv.at[u, 1])
        a_copies[1].start()
        a_side(u, 2).start()

    def group_size(g):
        us, jjs = FLAT[g][1]
        return len(us) * len(jjs)

    def rs_copy(g, d):
        span = pl.ds(FIRST[g], group_size(g))
        there = (x + d) % 4
        return send(
            part.at[there // 2, span, pl.ds((there % 2) * 2, 2)],
            sums.at[d - 1, span],
            rs_send.at[g, d - 1],
            rs_recv.at[g, d - 1],
            x_others[d - 1],
        )

    def groups_of(t):
        return [g for g, (when, _) in enumerate(FLAT) if when == t]

    def multiply(t):
        arrived(a_all.at[t, p, ya, pl.ds(0, 2)], af_recv.at[t, 0])
        arrived(a_all.at[t, p, ya, pl.ds(2, 2)], af_recv.at[t, 1])
        a_side(t, 3).start()
        arrived(b_all.at[t, za, pl.ds(0, 4)], bf_recv.at[t, 0])
        arrived(b_all.at[t, za, pl.ds(4, 4)], bf_recv.at[t, 1])
        for n, place in enumerate((y, ym, yp, ya)):
            arrived(a_all.at[t, 1 - p, place], as_recv.at[t, n])
        for g in groups_of(t):
            us, jjs = FLAT[g][1]
            for u in us:
                acc = None
                for s in range(4):
                    left = jnp.concatenate(
                        [a_all[u, :, s, :, k].reshape(8 * ROWS, 128) for k in range(8)], axis=1
                    )
                    right = jnp.concatenate([b_all[jj, s].reshape(1024, 128) for jj in jjs], axis=1)
                    product = jnp.dot(left, right, preferred_element_type=F32)
                    acc = product if acc is None else acc + product
                for n, jj in enumerate(jjs):
                    part[:, PLACE[u, jj]] = acc[:, n * 128 : (n + 1) * 128].reshape(2, 4, ROWS, 128)
            for d in (2, 1, 3):
                rs_copy(g, d).start()

    def span_of(r):
        return pl.ds(RUNS[r][1], RUNS[r][2])

    def mirror_remote(r):
        there = dev(2 * p + (RUNS[r][3] + p) % 2, z, y, h)
        return send(total.at[span_of(r)], mirror.at[l, span_of(r)], t_send.at[r], t_recv.at[r, l], there)

    def mirror_local(r):
        return pltpu.make_async_copy(total.at[span_of(r)], mirror.at[l, span_of(r)], t_recv.at[r, l])

    def mirror_here(r):
        return jnp.logical_and(on_self, (RUNS[r][3] + p) % 2 == l)

    def reduce(t):
        for g in groups_of(t):
            for d in (1, 3, 2):
                arrived(sums.at[d - 1, pl.ds(FIRST[g], group_size(g))], rs_recv.at[g, d - 1])
            us, jjs = FLAT[g][1]
            for jj in jjs:
                for u in us:
                    e = PLACE[u, jj]
                    value = part[h, e, pl.ds(2 * l, 2)] + sums[0, e] + sums[1, e] + sums[2, e]
                    total[e] = value
                    out[:, j_of(jj), pl.ds(u * ROWS, ROWS), :] = value
            for r, run in enumerate(RUNS):
                if run[0] == g:
                    @pl.when(mirror_here(r))
                    def _(r=r):
                        mirror_local(r).start()

                    @pl.when(jnp.logical_not(mirror_here(r)))
                    def _(r=r):
                        mirror_remote(r).start()

    own(0)
    own(1)
    for t in range(CHUNKS):
        forward(t)
        if t + 2 < CHUNKS:
            own(t + 2)
        if t >= 1:
            multiply(t - 1)
        if t >= 2:
            reduce(t - 2)
    multiply(CHUNKS - 1)
    reduce(CHUNKS - 2)
    reduce(CHUNKS - 1)

    for half in (0, 1):
        @pl.when((l + h) % 2 == half)
        def _(half=half):
            for r, run in enumerate(RUNS):
                if run[3] == half:
                    for n in (0, 1):
                        arrived(mirror.at[n, span_of(r)], t_recv.at[r, n])
            for i in (0, 1):
                for n in (0, 1):
                    for m in (0, 1):
                        tile = jnp.concatenate(
                            [mirror[n, PLACE[u, 2 * i + half], m] for u in range(CHUNKS)], axis=0
                        )
                        out[i, 2 * n + m] = out[i, 2 * n + m] + tile.T

    for t in range(CHUNKS):
        for copy in a_near(t) + b_near(t) + a_far(t) + b_far(t):
            copy.wait_send()
        for n in range(4):
            a_side(t, n).wait_send()
    for g in range(len(FLAT)):
        for d in (1, 2, 3):
            rs_copy(g, d).wait_send()
    for r in range(len(RUNS)):
        @pl.when(jnp.logical_not(mirror_here(r)))
        def _(r=r):
            mirror_remote(r).wait_send()

    @pl.when(swaps)
    def _():
        for u in range(CHUNKS):
            swap(u).wait_send()


def per_device(amplitudes, integrals):
    rows = integrals.reshape(8, 512, 128)
    dma = pltpu.SemaphoreType.DMA
    n = CHUNKS
    return pl.pallas_call(
        kernel,
        out_shape=jax.ShapeDtypeStruct((2, 4, 128, 128), F32),
        in_specs=[pl.BlockSpec(memory_space=pltpu.HBM)] * 2,
        out_specs=pl.BlockSpec(memory_space=pltpu.VMEM),
        scratch_shapes=[
            pltpu.VMEM((n, 2, 4, 4, 8, ROWS, 128), BF16),
            pltpu.VMEM((4, 4, 8, 128, 128), BF16),
            pltpu.VMEM((8, 512, 128), BF16),
            pltpu.VMEM((8, 512, 128), F32),
            pltpu.VMEM((2, n * n, 4, ROWS, 128), F32),
            pltpu.VMEM((3, n * n, 2, ROWS, 128), F32),
            pltpu.VMEM((n * n, 2, ROWS, 128), F32),
            pltpu.VMEM((2, n * n, 2, ROWS, 128), F32),
            dma, dma((n,)), dma((n,)),
            dma((n, 2)), dma((n, 2)), dma((n, 2)), dma((n, 2)), dma((n, 4)), dma((n, 4)),
            dma((n, 2)), dma((n, 2)), dma((n, 2)), dma((n, 2)),
            dma((len(FLAT), 3)), dma((len(FLAT), 3)), dma((len(RUNS),)), dma((len(RUNS), 2)),
        ],
        compiler_params=pltpu.CompilerParams(
            collective_id=0, has_side_effects=True, vmem_limit_bytes=62 << 20
        ),
        cost_estimate=pl.CostEstimate(flops=4 << 30, bytes_accessed=3 << 20, transcendentals=0),
        name="cycle_contraction",
    )(amplitudes, rows)


def solution(mesh):
    return jax.shard_map(
        per_device,
        mesh=mesh,
        in_specs=(P(None, "ka", "row", "col"), P("ka", "row", None, "col")),
        out_specs=P("ka", None, "row", "col"),
        check_vma=False,
    )
```

```python
import jax
import jax.numpy as jnp
from jax import lax
from jax.experimental import pallas as pl
from jax.experimental.pallas import tpu as pltpu
from jax.sharding import PartitionSpec as P

MESH = pl.DeviceIdType.MESH
CHUNKS = 4
ROWS = 32
F32 = jnp.float32
BF16 = jnp.bfloat16


GROUPS = [
    [((t,), (jj, jj + 1)[: t + 1 - jj]) for jj in range(0, t + 1, 2)] + ([(tuple(range(t)), (t,))] if t else [])
    for t in range(CHUNKS)
]
FLAT = [(t, group) for t in range(CHUNKS) for group in GROUPS[t]]
PLACE = {}
FIRST = []
for _, (us, jjs) in FLAT:
    FIRST.append(len(PLACE))
    for jj in jjs:
        for u in us:
            PLACE[u, jj] = len(PLACE)
RUNS = [
    (g, PLACE[us[0], jj], len(us), jj % 2)
    for g, (_, (us, jjs)) in enumerate(FLAT)
    for jj in jjs
]


GROUP_SIZE = [len(us) * len(jjs) for _, (us, jjs) in FLAT]
GROUP_ROW = [64 * FIRST[g] + 16 * g for g in range(len(FLAT))]
RUN_ROW = [64 * run[1] + 16 * r for r, run in enumerate(RUNS)]
GROUP_ROWS = 64 * CHUNKS**2 + 16 * len(FLAT)
RUN_ROWS = 64 * CHUNKS**2 + 16 * len(RUNS)


def encode(values, top):
    w = jnp.abs(values) * (255.0 / 16 / top) + 1.0 / 16
    w2 = w * w
    w4 = w2 * w2
    w8 = w4 * w4
    code = w8 * w8 * w8 * (w4 * w2 * w)
    return jnp.where(values < 0, -code, code).astype(BF16)


def decode(codes, top):
    codes = codes.astype(F32)
    w = jnp.exp2(jnp.log2(jnp.abs(codes)) * (1.0 / 31))
    size = (w - 1.0 / 16) * (top * (16.0 / 255))
    return jnp.where(codes < 0, -size, size)


def send(src, dst, send_sem, recv_sem, device):
    return pltpu.make_async_remote_copy(
        src_ref=src,
        dst_ref=dst,
        send_sem=send_sem,
        recv_sem=recv_sem,
        device_id=device,
        device_id_type=MESH,
    )


def arrived(ref, sem):
    pltpu.make_async_copy(ref, ref, sem).wait()


def kernel(
    a_in, b_in, out,
    a_all, b_all, b_raw, b_wide, part, part16, sums16, total, total16, mirror16,
    b_sem, a_ready, swap_send,
    an_send, an_recv, af_send, af_recv, as_send, as_recv,
    bn_send, bn_recv, bf_send, bf_recv,
    rs_send, rs_recv, t_send, t_recv,
):
    row, col, l = lax.axis_index("row"), lax.axis_index("col"), lax.axis_index("ka")
    z, h = row // 2, row % 2
    y, p = col // 2, col % 2
    x = 2 * h + l

    def dev(x, y, z, p):
        return (z * 2 + x // 2, y * 2 + p, x % 2)

    yp, ym, ya = (y + 1) % 4, (y + 3) % 4, (y + 2) % 4
    zp, zm, za = (z + 1) % 4, (z + 3) % 4, (z + 2) % 4
    y_next, y_prev = dev(x, yp, z, p), dev(x, ym, z, p)
    z_next, z_prev = dev(x, y, zp, p), dev(x, y, zm, p)
    sibling = dev(x, y, z, 1 - p)
    partner = dev((x + 2) % 4, y, z, 1 - p)
    x_others = [dev((x + d) % 4, y, z, p) for d in (1, 2, 3)]
    mirrors = [dev(2 * p + t, z, y, h) for t in (0, 1)]
    swaps = p != h
    on_self = jnp.logical_and(y == z, p == h)

    def j_of(jj):
        return ((jj % 2 + p) % 2) * 2 + jj // 2

    b_copy = pltpu.make_async_copy(b_in, b_raw, b_sem)
    b_copy.start()

    @pl.when(jnp.logical_not(swaps))
    def _():
        for u in range(CHUNKS):
            pltpu.make_async_copy(
                a_in.at[:, :, pl.ds(u * ROWS, ROWS), :], a_all.at[u, p, y], a_ready.at[u]
            ).start()

    barrier = pltpu.get_barrier_semaphore()

    def greet(device):
        pl.semaphore_signal(barrier, inc=1, device_id=device, device_id_type=MESH)

    for device in [y_next, y_prev, z_next, z_prev, sibling] + x_others:
        greet(device)

    @pl.when(swaps)
    def _():
        greet(partner)

    for t in (0, 1):
        @pl.when(jnp.logical_not(jnp.logical_and(on_self, l == t)))
        def _(t=t):
            greet(mirrors[t])

    b_copy.wait()
    for k in range(8):
        b_wide[k] = b_raw[k].astype(F32)
    for j in (0, 2, 1, 3):
        jj = (j % 2) * 2 + (j // 2 + p) % 2
        for k in range(8):
            b_all[jj, z, k] = b_wide[k, pl.ds(j, 128, stride=4), :].astype(BF16)

    peers = 9 + jnp.where(swaps, 1, 0) + jnp.where(on_self, 0, 1)
    pl.semaphore_wait(barrier, peers)

    def swap(u):
        return send(
            a_in.at[:, :, pl.ds(u * ROWS, ROWS), :],
            a_all.at[u, 1 - p, y],
            swap_send.at[u],
            a_ready.at[u],
            partner,
        )

    def start_swap(u):
        @pl.when(swaps)
        def _():
            swap(u).start()

    start_swap(0)
    start_swap(1)

    def a_piece(u, place, half):
        return a_all.at[u, p, place, pl.ds(2 * half, 2)]

    def b_piece(u, place, half):
        return b_all.at[u, place, pl.ds(4 * half, 4)]

    def a_near(u, way, half):
        piece = a_piece(u, y, half)
        return send(piece, piece, an_send.at[u, way, half], an_recv.at[u, way, half], (y_next, y_prev)[way])

    def b_near(u, way, half):
        piece = b_piece(u, z, half)
        return send(piece, piece, bn_send.at[u, way, half], bn_recv.at[u, way, half], (z_next, z_prev)[way])

    def a_far(u, way):
        piece = a_piece(u, (ym, yp)[way], way)
        return send(piece, piece, af_send.at[u, way], af_recv.at[u, way], (y_next, y_prev)[way])

    def b_far(u, way):
        piece = b_piece(u, (zm, zp)[way], way)
        return send(piece, piece, bf_send.at[u, way], bf_recv.at[u, way], (z_next, z_prev)[way])

    def a_side(u, n):
        slot = a_all.at[u, p, (y, ym, yp, ya)[n]]
        return send(slot, slot, as_send.at[u, n], as_recv.at[u, n], sibling)

    def own_first(u):
        b_near(u, 0, 0).start()
        b_near(u, 1, 1).start()
        arrived(a_all.at[u, p, y], a_ready.at[u])
        a_near(u, 0, 0).start()
        a_near(u, 1, 1).start()
        a_side(u, 0).start()
        if u + 2 < CHUNKS:
            start_swap(u + 2)

    def own_second(u):
        for way in (0, 1):
            b_near(u, way, 1 - way).start()
            a_near(u, way, 1 - way).start()

    def first(u):
        for way in (0, 1):
            arrived(b_piece(u, (zm, zp)[way], way), bn_recv.at[u, way, way])
            b_far(u, way).start()
        for way in (0, 1):
            arrived(a_piece(u, (ym, yp)[way], way), an_recv.at[u, way, way])
            a_far(u, way).start()

    def second(u):
        for way in (0, 1):
            arrived(b_piece(u, (zm, zp)[way], 1 - way), bn_recv.at[u, way, 1 - way])
            arrived(a_piece(u, (ym, yp)[way], 1 - way), an_recv.at[u, way, 1 - way])
            a_side(u, 1 + way).start()

    def rs_copy(g, d):
        span = pl.ds(GROUP_ROW[g], 64 * GROUP_SIZE[g] + 16)
        there = (x + d) % 4
        return send(
            part16.at[there // 2, there % 2, span],
            sums16.at[d - 1, span],
            rs_send.at[g, d - 1],
            rs_recv.at[g, d - 1],
            x_others[d - 1],
        )

    def groups_of(t):
        return [g for g, (when, _) in enumerate(FLAT) if when == t]

    def multiply(t):
        arrived(a_all.at[t, p, ya, pl.ds(0, 2)], af_recv.at[t, 0])
        arrived(a_all.at[t, p, ya, pl.ds(2, 2)], af_recv.at[t, 1])
        a_side(t, 3).start()
        arrived(b_all.at[t, za, pl.ds(0, 4)], bf_recv.at[t, 0])
        arrived(b_all.at[t, za, pl.ds(4, 4)], bf_recv.at[t, 1])
        for n, place in enumerate((y, ym, yp, ya)):
            arrived(a_all.at[t, 1 - p, place], as_recv.at[t, n])
        for g in groups_of(t):
            us, jjs = FLAT[g][1]
            top = jnp.full((1, 128), 1e-30, F32)
            for u in us:
                acc = None
                for s in range(4):
                    left = jnp.concatenate(
                        [a_all[u, :, s, :, k].reshape(8 * ROWS, 128) for k in range(8)], axis=1
                    )
                    right = jnp.concatenate([b_all[jj, s].reshape(1024, 128) for jj in jjs], axis=1)
                    product = jnp.dot(left, right, preferred_element_type=F32)
                    acc = product if acc is None else acc + product
                for n, jj in enumerate(jjs):
                    block = acc[:, n * 128 : (n + 1) * 128]
                    top = jnp.maximum(top, jnp.max(jnp.abs(block), axis=0, keepdims=True))
                    part[:, PLACE[u, jj]] = block.reshape(2, 2, 2 * ROWS, 128)
            top16 = top.astype(BF16)
            top = top16.astype(F32)
            for n in range(GROUP_SIZE[g]):
                part16[:, :, pl.ds(GROUP_ROW[g] + 64 * n, 64)] = encode(part[:, FIRST[g] + n], top)
            part16[:, :, pl.ds(GROUP_ROW[g] + 64 * GROUP_SIZE[g], 16)] = jnp.broadcast_to(top16, (2, 2, 16, 128))
            for d in (2, 1, 3):
                rs_copy(g, d).start()

    def run_span(r):
        return pl.ds(RUN_ROW[r], 64 * RUNS[r][2] + 16)

    def mirror_remote(r):
        there = dev(2 * p + (RUNS[r][3] + p) % 2, z, y, h)
        return send(total16.at[run_span(r)], mirror16.at[l, run_span(r)], t_send.at[r], t_recv.at[r, l], there)

    def mirror_local(r):
        return pltpu.make_async_copy(total16.at[run_span(r)], mirror16.at[l, run_span(r)], t_recv.at[r, l])

    def mirror_here(r):
        return jnp.logical_and(on_self, (RUNS[r][3] + p) % 2 == l)

    def reduce(t):
        for g in groups_of(t):
            tops = []
            for d in (0, 2, 1):
                arrived(sums16.at[d, pl.ds(GROUP_ROW[g], 64 * GROUP_SIZE[g] + 16)], rs_recv.at[g, d])
            for d in range(3):
                tops.append(sums16[d, pl.ds(GROUP_ROW[g] + 64 * GROUP_SIZE[g], 16)].astype(F32)[:1])
            for r, (group, place, count, _) in enumerate(RUNS):
                if group != g:
                    continue
                jj = FLAT[g][1][1][(place - FIRST[g]) // count]
                top = jnp.full((1, 128), 1e-30, F32)
                for n, u in enumerate(FLAT[g][1][0]):
                    value = part[h, place + n, l]
                    for d in range(3):
                        row = GROUP_ROW[g] + 64 * (place - FIRST[g] + n)
                        value = value + decode(sums16[d, pl.ds(row, 64)], tops[d])
                    total[place + n] = value
                    top = jnp.maximum(top, jnp.max(jnp.abs(value), axis=0, keepdims=True))
                    out[:, j_of(jj), pl.ds(u * ROWS, ROWS), :] = value.reshape(2, ROWS, 128)
                top16 = top.astype(BF16)
                top = top16.astype(F32)
                for n in range(count):
                    total16[pl.ds(RUN_ROW[r] + 64 * n, 64)] = encode(total[place + n], top)
                total16[pl.ds(RUN_ROW[r] + 64 * count, 16)] = jnp.broadcast_to(top16, (16, 128))

                @pl.when(mirror_here(r))
                def _(r=r):
                    mirror_local(r).start()

                @pl.when(jnp.logical_not(mirror_here(r)))
                def _(r=r):
                    mirror_remote(r).start()

    own_first(0)
    own_second(0)
    for t in range(CHUNKS):
        if t >= 1:
            multiply(t - 1)
        first(t)
        if t + 1 < CHUNKS:
            own_first(t + 1)
        second(t)
        if t + 1 < CHUNKS:
            own_second(t + 1)
        if t >= 1:
            reduce(t - 1)
    multiply(CHUNKS - 1)
    reduce(CHUNKS - 1)

    for half in (0, 1):
        @pl.when((l + h) % 2 == half)
        def _(half=half):
            for r, run in enumerate(RUNS):
                if run[3] == half:
                    for n in (0, 1):
                        arrived(mirror16.at[n, run_span(r)], t_recv.at[r, n])
            where = {}
            for r, (g, _, count, _) in enumerate(RUNS):
                jj = FLAT[g][1][1][(RUNS[r][1] - FIRST[g]) // count]
                for n, u in enumerate(FLAT[g][1][0]):
                    where[u, jj] = RUN_ROW[r] + 64 * n, RUN_ROW[r] + 64 * count
            for i in (0, 1):
                for n in (0, 1):
                    pieces = []
                    for u in range(CHUNKS):
                        row, top_row = where[u, 2 * i + half]
                        top = mirror16[n, pl.ds(top_row, 16)].astype(F32)[:1]
                        pieces.append(decode(mirror16[n, pl.ds(row, 64)], top))
                    for m in (0, 1):
                        tile = jnp.concatenate([piece[m * ROWS : (m + 1) * ROWS] for piece in pieces], axis=0)
                        out[i, 2 * n + m] = out[i, 2 * n + m] + tile.T

    for t in range(CHUNKS):
        for way in (0, 1):
            for half in (0, 1):
                a_near(t, way, half).wait_send()
                b_near(t, way, half).wait_send()
            a_far(t, way).wait_send()
            b_far(t, way).wait_send()
        for n in range(4):
            a_side(t, n).wait_send()
    for g in range(len(FLAT)):
        for d in (1, 2, 3):
            rs_copy(g, d).wait_send()
    for r in range(len(RUNS)):
        @pl.when(jnp.logical_not(mirror_here(r)))
        def _(r=r):
            mirror_remote(r).wait_send()

    @pl.when(swaps)
    def _():
        for u in range(CHUNKS):
            swap(u).wait_send()


def per_device(amplitudes, integrals):
    rows = integrals.reshape(8, 512, 128)
    dma = pltpu.SemaphoreType.DMA
    n = CHUNKS
    return pl.pallas_call(
        kernel,
        out_shape=jax.ShapeDtypeStruct((2, 4, 128, 128), F32),
        in_specs=[pl.BlockSpec(memory_space=pltpu.HBM)] * 2,
        out_specs=pl.BlockSpec(memory_space=pltpu.VMEM),
        scratch_shapes=[
            pltpu.VMEM((n, 2, 4, 4, 8, ROWS, 128), BF16),
            pltpu.VMEM((4, 4, 8, 128, 128), BF16),
            pltpu.VMEM((8, 512, 128), BF16),
            pltpu.VMEM((8, 512, 128), F32),
            pltpu.VMEM((2, n * n, 2, 2 * ROWS, 128), F32),
            pltpu.VMEM((2, 2, GROUP_ROWS, 128), BF16),
            pltpu.VMEM((3, GROUP_ROWS, 128), BF16),
            pltpu.VMEM((n * n, 2 * ROWS, 128), F32),
            pltpu.VMEM((RUN_ROWS, 128), BF16),
            pltpu.VMEM((2, RUN_ROWS, 128), BF16),
            dma, dma((n,)), dma((n,)),
            dma((n, 2, 2)), dma((n, 2, 2)), dma((n, 2)), dma((n, 2)), dma((n, 4)), dma((n, 4)),
            dma((n, 2, 2)), dma((n, 2, 2)), dma((n, 2)), dma((n, 2)),
            dma((len(FLAT), 3)), dma((len(FLAT), 3)), dma((len(RUNS),)), dma((len(RUNS), 2)),
        ],
        compiler_params=pltpu.CompilerParams(
            collective_id=0, has_side_effects=True, vmem_limit_bytes=62 << 20
        ),
        cost_estimate=pl.CostEstimate(flops=4 << 30, bytes_accessed=3 << 20, transcendentals=0),
        name="cycle_contraction",
    )(amplitudes, rows)


def solution(mesh):
    return jax.shard_map(
        per_device,
        mesh=mesh,
        in_specs=(P(None, "ka", "row", "col"), P("ka", "row", None, "col")),
        out_specs=P("ka", None, "row", "col"),
        check_vma=False,
    )
```

```python
import jax
import jax.numpy as jnp
from jax import lax
from jax.experimental import pallas as pl
from jax.experimental.pallas import tpu as pltpu
from jax.sharding import PartitionSpec as P

MESH = pl.DeviceIdType.MESH
CHUNKS = 4
SIZES = (32, 48, 32, 16)
STARTS = tuple(sum(SIZES[:u]) for u in range(CHUNKS))
F32 = jnp.float32
BF16 = jnp.bfloat16


GROUPS = [
    [((t,), (jj, jj + 1)[: t + 1 - jj]) for jj in range(0, t + 1, 2)] + ([(tuple(range(t)), (t,))] if t else [])
    for t in range(CHUNKS)
]
FLAT = [(t, group) for t in range(CHUNKS) for group in GROUPS[t]]
RUNS = [(g, us, jj) for g, (_, (us, jjs)) in enumerate(FLAT) for jj in jjs]


def layout(parts, pad):
    rows, spans, at = {}, [], 0
    for blocks in parts:
        first = at
        for u, jj in blocks:
            rows[u, jj] = at
            at += 2 * SIZES[u]
        spans.append((first, at - first + pad))
        at += pad
    return rows, spans, at


GROUP_BLOCKS = [[(u, jj) for jj in jjs for u in us] for _, (us, jjs) in FLAT]
RUN_BLOCKS = [[(u, jj) for u in us] for _, us, jj in RUNS]
PLAIN, _, PLAIN_ROWS = layout(GROUP_BLOCKS, 0)
GROUP_ROW, GROUP_SPAN, GROUP_ROWS = layout(GROUP_BLOCKS, 16)
RUN_ROW, RUN_SPAN, RUN_ROWS = layout(RUN_BLOCKS, 16)


def encode(values, top):
    w = jnp.abs(values) * (255.0 / 16 / top) + 1.0 / 16
    w2 = w * w
    w4 = w2 * w2
    w8 = w4 * w4
    code = w8 * w8 * w8 * (w4 * w2 * w)
    return jnp.where(values < 0, -code, code).astype(BF16)


def decode(codes, top):
    codes = codes.astype(F32)
    w = jnp.exp2(jnp.log2(jnp.abs(codes)) * (1.0 / 31))
    size = (w - 1.0 / 16) * (top * (16.0 / 255))
    return jnp.where(codes < 0, -size, size)


def send(src, dst, send_sem, recv_sem, device):
    return pltpu.make_async_remote_copy(
        src_ref=src,
        dst_ref=dst,
        send_sem=send_sem,
        recv_sem=recv_sem,
        device_id=device,
        device_id_type=MESH,
    )


def arrived(ref, sem):
    pltpu.make_async_copy(ref, ref, sem).wait()


def kernel(
    a_in, b_in, out,
    a_0, a_1, a_2, a_3, v_0, v_1, v_2, v_3, b_all, b_raw, b_wide, part, part16, sums16, total, total16, mirror16,
    b_sem, a_ready, swap_send, side_send, side_recv,
    an_send, an_recv, af_send, af_recv, as_send, as_recv,
    bn_send, bn_recv, bf_send, bf_recv,
    rs_send, rs_recv, t_send, t_recv,
):
    a_all, via = (a_0, a_1, a_2, a_3), (v_0, v_1, v_2, v_3)
    row, col, l = lax.axis_index("row"), lax.axis_index("col"), lax.axis_index("ka")
    z, h = row // 2, row % 2
    y, p = col // 2, col % 2
    x = 2 * h + l

    def dev(x, y, z, p):
        return (z * 2 + x // 2, y * 2 + p, x % 2)

    yp, ym, ya = (y + 1) % 4, (y + 3) % 4, (y + 2) % 4
    zp, zm, za = (z + 1) % 4, (z + 3) % 4, (z + 2) % 4
    y_next, y_prev = dev(x, yp, z, p), dev(x, ym, z, p)
    z_next, z_prev = dev(x, y, zp, p), dev(x, y, zm, p)
    sibling = dev(x, y, z, 1 - p)
    partner = dev((x + 2) % 4, y, z, 1 - p)
    x_others = [dev((x + d) % 4, y, z, p) for d in (1, 2, 3)]
    mirrors = [dev(2 * p + t, z, y, h) for t in (0, 1)]
    swaps = p != h
    on_self = jnp.logical_and(y == z, p == h)

    def j_of(jj):
        return ((jj % 2 + p) % 2) * 2 + jj // 2

    b_copy = pltpu.make_async_copy(b_in, b_raw, b_sem)
    b_copy.start()

    def a_part(u, half):
        return a_in.at[pl.ds(2 * half, 2), :, pl.ds(STARTS[u], SIZES[u]), :]

    @pl.when(jnp.logical_not(swaps))
    def _():
        for u in range(CHUNKS):
            for half in (0, 1):
                pltpu.make_async_copy(
                    a_part(u, half), a_all[u].at[p, y, pl.ds(2 * half, 2)], a_ready.at[u, half]
                ).start()

    barrier = pltpu.get_barrier_semaphore()

    def greet(device):
        pl.semaphore_signal(barrier, inc=1, device_id=device, device_id_type=MESH)

    for device in [y_next, y_prev, z_next, z_prev, sibling] + x_others:
        greet(device)

    @pl.when(swaps)
    def _():
        greet(partner)

    for t in (0, 1):
        @pl.when(jnp.logical_not(jnp.logical_and(on_self, l == t)))
        def _(t=t):
            greet(mirrors[t])

    def relayout(js):
        for j in js:
            jj = (j % 2) * 2 + (j // 2 + p) % 2
            for k in range(8):
                b_all[jj, z, k] = b_wide[k, pl.ds(j, 128, stride=4), :].astype(BF16)

    b_copy.wait()
    for k in range(8):
        b_wide[k] = b_raw[k].astype(F32)
    relayout((0, 2))

    peers = 9 + jnp.where(swaps, 1, 0) + jnp.where(on_self, 0, 1)
    pl.semaphore_wait(barrier, peers)

    def swap(u):
        return send(
            a_part(u, 0), a_all[u].at[1 - p, y, pl.ds(0, 2)], swap_send.at[u], a_ready.at[u, 0], partner
        )

    def swap_side(u):
        return send(a_part(u, 1), via[u], side_send.at[u], side_recv.at[u], sibling)

    def swap_on(u):
        return send(
            via[u], a_all[u].at[p, y, pl.ds(2, 2)], swap_send.at[u], a_ready.at[u, 1], x_others[1]
        )

    @pl.when(swaps)
    def _():
        for u in range(CHUNKS):
            swap_side(u).start()
            swap(u).start()

    def a_piece(u, place, half):
        return a_all[u].at[p, place, pl.ds(2 * half, 2)]

    def b_piece(u, place, half):
        return b_all.at[u, place, pl.ds(4 * half, 4)]

    def a_near(u, way, half):
        piece = a_piece(u, y, half)
        return send(piece, piece, an_send.at[u, way, half], an_recv.at[u, way, half], (y_next, y_prev)[way])

    def b_near(u, way, half):
        piece = b_piece(u, z, half)
        return send(piece, piece, bn_send.at[u, way, half], bn_recv.at[u, way, half], (z_next, z_prev)[way])

    def a_far(u, way):
        piece = a_piece(u, (ym, yp)[way], way)
        return send(piece, piece, af_send.at[u, way], af_recv.at[u, way], (y_next, y_prev)[way])

    def b_far(u, way):
        piece = b_piece(u, (zm, zp)[way], way)
        return send(piece, piece, bf_send.at[u, way], bf_recv.at[u, way], (z_next, z_prev)[way])

    def a_side(u, n):
        slot = a_all[u].at[p, (y, ym, yp, ya)[n]]
        return send(slot, slot, as_send.at[u, n], as_recv.at[u, n], sibling)

    def b_first(u):
        b_near(u, 0, 0).start()
        b_near(u, 1, 1).start()

    def b_second(u):
        b_near(u, 0, 1).start()
        b_near(u, 1, 0).start()

    def a_first(u):
        for half in (0, 1):
            arrived(a_piece(u, y, half), a_ready.at[u, half])
        a_near(u, 0, 0).start()
        a_near(u, 1, 1).start()

    def a_second(u):
        a_near(u, 0, 1).start()
        a_near(u, 1, 0).start()
        a_side(u, 0).start()

    def first(u):
        for way in (0, 1):
            arrived(b_piece(u, (zm, zp)[way], way), bn_recv.at[u, way, way])
            b_far(u, way).start()
        if u + 1 < CHUNKS:
            b_second(u + 1)
        for way in (0, 1):
            arrived(a_piece(u, (ym, yp)[way], way), an_recv.at[u, way, way])
            a_far(u, way).start()
        if u + 1 < CHUNKS:
            a_second(u + 1)

    def second(u):
        for way in (0, 1):
            arrived(b_piece(u, (zm, zp)[way], 1 - way), bn_recv.at[u, way, 1 - way])
        if u + 2 < CHUNKS:
            b_first(u + 2)
        for way in (0, 1):
            arrived(a_piece(u, (ym, yp)[way], 1 - way), an_recv.at[u, way, 1 - way])
            a_side(u, 1 + way).start()
        if u + 2 < CHUNKS:
            a_first(u + 2)

    def rs_copy(g, d):
        span = pl.ds(*GROUP_SPAN[g])
        there = (x + d) % 4
        return send(
            part16.at[there // 2, there % 2, span],
            sums16.at[d - 1, span],
            rs_send.at[g, d - 1],
            rs_recv.at[g, d - 1],
            x_others[d - 1],
        )

    def groups_of(t):
        return [g for g, (when, _) in enumerate(FLAT) if when == t]

    def product(u, jjs, places):
        total = None
        for s in places:
            left = jnp.concatenate(
                [a_all[u][:, s, :, k].reshape(8 * SIZES[u], 128) for k in range(8)], axis=1
            )
            right = jnp.concatenate([b_all[jj, s].reshape(1024, 128) for jj in jjs], axis=1)
            one = jnp.dot(left, right, preferred_element_type=F32)
            total = one if total is None else total + one
        return total

    def put(g, u, jjs, value, add):
        size = 2 * SIZES[u]
        tops = []
        for n, jj in enumerate(jjs):
            block = value[:, n * 128 : (n + 1) * 128]
            at = pl.ds(PLAIN[u, jj], size)
            if add:
                block = block + part[:, :, at].reshape(4 * size, 128)
            part[:, :, at] = block.reshape(2, 2, size, 128)
            tops.append(jnp.max(jnp.abs(block), axis=0, keepdims=True))
        return tops

    def send_group(g, tops):
        top = jnp.full((1, 128), 1e-30, F32)
        for one in tops:
            top = jnp.maximum(top, one)
        top16 = top.astype(BF16)
        top = top16.astype(F32)
        for u, jj in GROUP_BLOCKS[g]:
            size = 2 * SIZES[u]
            part16[:, :, pl.ds(GROUP_ROW[u, jj], size)] = encode(part[:, :, pl.ds(PLAIN[u, jj], size)], top)
        end = sum(GROUP_SPAN[g])
        part16[:, :, pl.ds(end - 16, 16)] = jnp.broadcast_to(top16, (2, 2, 16, 128))
        for d in (2, 1, 3):
            rs_copy(g, d).start()

    def side_arrived(t, n):
        arrived(a_all[t].at[1 - p, (y, ym, yp, ya)[n]], as_recv.at[t, n])

    def far(t):
        for way in (0, 1):
            arrived(a_piece(t, ya, way), af_recv.at[t, way])
        a_side(t, 3).start()
        for way in (0, 1):
            arrived(b_piece(t, za, way), bf_recv.at[t, way])

    def early(t):
        for n in range(3):
            side_arrived(t, n)
        for g in reversed(groups_of(t)):
            us, jjs = FLAT[g][1]
            if us == (t,) and t not in jjs:
                put(g, t, jjs, product(t, jjs, (y, ym, yp)), False)
            elif us != (t,):
                for u in us:
                    put(g, u, jjs, product(u, jjs, (z, zm, zp)), False)

    def late(t):
        far(t)
        side = True
        for g in reversed(groups_of(t)):
            us, jjs = FLAT[g][1]
            tops = []
            if us == (t,) and side:
                side_arrived(t, 3)
                side = False
            if us != (t,):
                for u in us:
                    tops += put(g, u, jjs, product(u, jjs, (za,)), True)
            else:
                if t in jjs:
                    tops += put(g, t, jjs, product(t, jjs, range(4)), False)
                else:
                    tops += put(g, t, jjs, product(t, jjs, (ya,)), True)
            send_group(g, tops)

    def run_span(r):
        return pl.ds(*RUN_SPAN[r])

    def mirror_remote(r):
        there = dev(2 * p + (RUNS[r][2] + p) % 2, z, y, h)
        return send(total16.at[run_span(r)], mirror16.at[l, run_span(r)], t_send.at[r], t_recv.at[r, l], there)

    def mirror_local(r):
        return pltpu.make_async_copy(total16.at[run_span(r)], mirror16.at[l, run_span(r)], t_recv.at[r, l])

    def mirror_here(r):
        return jnp.logical_and(on_self, (RUNS[r][2] + p) % 2 == l)

    def top_of(ref, end):
        return ref[pl.ds(end - 16, 16)].astype(F32)[:1]

    def reduce(t):
        for g in reversed(groups_of(t)):
            for d in (0, 2, 1):
                arrived(sums16.at[d, pl.ds(*GROUP_SPAN[g])], rs_recv.at[g, d])
            tops = [top_of(sums16.at[d], sum(GROUP_SPAN[g])) for d in range(3)]
            for r, (group, us, jj) in enumerate(RUNS):
                if group != g:
                    continue
                top = jnp.full((1, 128), 1e-30, F32)
                for u in us:
                    size = 2 * SIZES[u]
                    value = part[h, l, pl.ds(PLAIN[u, jj], size)]
                    for d in range(3):
                        value = value + decode(sums16[d, pl.ds(GROUP_ROW[u, jj], size)], tops[d])
                    total[pl.ds(PLAIN[u, jj], size)] = value
                    top = jnp.maximum(top, jnp.max(jnp.abs(value), axis=0, keepdims=True))
                    out[:, j_of(jj), pl.ds(STARTS[u], SIZES[u]), :] = value.reshape(2, SIZES[u], 128)
                top16 = top.astype(BF16)
                top = top16.astype(F32)
                for u in us:
                    size = 2 * SIZES[u]
                    total16[pl.ds(RUN_ROW[u, jj], size)] = encode(total[pl.ds(PLAIN[u, jj], size)], top)
                total16[pl.ds(sum(RUN_SPAN[r]) - 16, 16)] = jnp.broadcast_to(top16, (16, 128))

                @pl.when(mirror_here(r))
                def _(r=r):
                    mirror_local(r).start()

                @pl.when(jnp.logical_not(mirror_here(r)))
                def _(r=r):
                    mirror_remote(r).start()

    def sums_left(t):
        for g in groups_of(t):
            for d in (1, 2, 3):
                rs_copy(g, d).wait_send()

    def rings_left():
        for t in range(CHUNKS):
            for way in (0, 1):
                for half in (0, 1):
                    a_near(t, way, half).wait_send()
                    b_near(t, way, half).wait_send()
                a_far(t, way).wait_send()
                b_far(t, way).wait_send()
            for n in range(4):
                a_side(t, n).wait_send()

        @pl.when(swaps)
        def _():
            for u in range(CHUNKS):
                swap_side(u).wait_send()
                swap(u).wait_send()

        @pl.when(jnp.logical_not(swaps))
        def _():
            for u in range(CHUNKS):
                swap_on(u).wait_send()

    last = CHUNKS - 1
    b_first(0)
    b_second(0)
    b_first(1)

    @pl.when(jnp.logical_not(swaps))
    def _():
        a_first(0)
        a_second(0)
        a_first(1)
        for u in range(CHUNKS):
            arrived(via[u], side_recv.at[u])
            swap_on(u).start()

    relayout((1, 3))

    @pl.when(swaps)
    def _():
        a_first(0)
        a_second(0)
        a_first(1)

    for t in range(CHUNKS):
        first(t)
        second(t)
        early(t)
        if t >= 1:
            reduce(t - 1)
        late(t)
    rings_left()
    for t in range(last):
        sums_left(t)
    reduce(last)
    sums_left(last)

    for half in (0, 1):
        @pl.when((l + h) % 2 == half)
        def _(half=half):
            for r, (_, _, jj) in enumerate(RUNS):
                if jj % 2 == half:
                    for n in (0, 1):
                        arrived(mirror16.at[n, run_span(r)], t_recv.at[r, n])
            for i in (0, 1):
                jj = 2 * i + half
                for n in (0, 1):
                    pieces = []
                    for u in range(CHUNKS):
                        (r,) = [r for r, (_, us, at) in enumerate(RUNS) if u in us and at == jj]
                        top = top_of(mirror16.at[n], sum(RUN_SPAN[r]))
                        pieces.append(decode(mirror16[n, pl.ds(RUN_ROW[u, jj], 2 * SIZES[u])], top))
                    for m in (0, 1):
                        tile = jnp.concatenate(
                            [piece[m * SIZES[u] : (m + 1) * SIZES[u]] for u, piece in enumerate(pieces)], axis=0
                        )
                        out[i, 2 * n + m] = out[i, 2 * n + m] + tile.T

    for r in range(len(RUNS)):
        @pl.when(jnp.logical_not(mirror_here(r)))
        def _(r=r):
            mirror_remote(r).wait_send()


def per_device(amplitudes, integrals):
    rows = integrals.reshape(8, 512, 128)
    dma = pltpu.SemaphoreType.DMA
    n = CHUNKS
    return pl.pallas_call(
        kernel,
        out_shape=jax.ShapeDtypeStruct((2, 4, 128, 128), F32),
        in_specs=[pl.BlockSpec(memory_space=pltpu.HBM)] * 2,
        out_specs=pl.BlockSpec(memory_space=pltpu.VMEM),
        scratch_shapes=[
            *[pltpu.VMEM((2, 4, 4, 8, size, 128), BF16) for size in SIZES],
            *[pltpu.VMEM((2, 8, size, 128), BF16) for size in SIZES],
            pltpu.VMEM((4, 4, 8, 128, 128), BF16),
            pltpu.VMEM((8, 512, 128), BF16),
            pltpu.VMEM((8, 512, 128), F32),
            pltpu.VMEM((2, 2, PLAIN_ROWS, 128), F32),
            pltpu.VMEM((2, 2, GROUP_ROWS, 128), BF16),
            pltpu.VMEM((3, GROUP_ROWS, 128), BF16),
            pltpu.VMEM((PLAIN_ROWS, 128), F32),
            pltpu.VMEM((RUN_ROWS, 128), BF16),
            pltpu.VMEM((2, RUN_ROWS, 128), BF16),
            dma, dma((n, 2)), dma((n,)), dma((n,)), dma((n,)),
            dma((n, 2, 2)), dma((n, 2, 2)), dma((n, 2)), dma((n, 2)), dma((n, 4)), dma((n, 4)),
            dma((n, 2, 2)), dma((n, 2, 2)), dma((n, 2)), dma((n, 2)),
            dma((len(FLAT), 3)), dma((len(FLAT), 3)), dma((len(RUNS),)), dma((len(RUNS), 2)),
        ],
        compiler_params=pltpu.CompilerParams(
            collective_id=0, has_side_effects=True, vmem_limit_bytes=62 << 20
        ),
        cost_estimate=pl.CostEstimate(flops=4 << 30, bytes_accessed=3 << 20, transcendentals=0),
        name="cycle_contraction",
    )(amplitudes, rows)


def solution(mesh):
    return jax.shard_map(
        per_device,
        mesh=mesh,
        in_specs=(P(None, "ka", "row", "col"), P("ka", "row", None, "col")),
        out_specs=P("ka", None, "row", "col"),
        check_vma=False,
    )
```

```python
import jax
import jax.numpy as jnp
from jax import lax
from jax.experimental import pallas as pl
from jax.experimental.pallas import tpu as pltpu
from jax.sharding import PartitionSpec as P

MESH = pl.DeviceIdType.MESH
CHUNKS = 4
SIZES = (32, 48, 32, 16)
STARTS = tuple(sum(SIZES[:u]) for u in range(CHUNKS))
F32 = jnp.float32
BF16 = jnp.bfloat16


GROUPS = [
    [((t,), (jj, jj + 1)[: t + 1 - jj]) for jj in range(0, t + 1, 2)] + ([(tuple(range(t)), (t,))] if t else [])
    for t in range(CHUNKS)
]
FLAT = [(t, group) for t in range(CHUNKS) for group in GROUPS[t]]
RUNS = [(g, us, jj) for g, (_, (us, jjs)) in enumerate(FLAT) for jj in jjs]


def layout(parts, pad):
    rows, spans, at = {}, [], 0
    for blocks in parts:
        first = at
        for u, jj in blocks:
            rows[u, jj] = at
            at += 2 * SIZES[u]
        spans.append((first, at - first + pad))
        at += pad
    return rows, spans, at


GROUP_BLOCKS = [[(u, jj) for jj in jjs for u in us] for _, (us, jjs) in FLAT]
RUN_BLOCKS = [[(u, jj) for u in us] for _, us, jj in RUNS]
PLAIN, _, PLAIN_ROWS = layout(GROUP_BLOCKS, 0)
GROUP_ROW, GROUP_SPAN, GROUP_ROWS = layout(GROUP_BLOCKS, 16)
RUN_ROW, RUN_SPAN, RUN_ROWS = layout(RUN_BLOCKS, 16)


def encode(values, top):
    w = jnp.abs(values) * (255.0 / 16 / top) + 1.0 / 16
    w2 = w * w
    w4 = w2 * w2
    w8 = w4 * w4
    code = w8 * w8 * w8 * (w4 * w2 * w)
    return jnp.where(values < 0, -code, code).astype(BF16)


def decode(codes, top):
    codes = codes.astype(F32)
    w = jnp.exp2(jnp.log2(jnp.abs(codes)) * (1.0 / 31))
    size = (w - 1.0 / 16) * (top * (16.0 / 255))
    return jnp.where(codes < 0, -size, size)


def send(src, dst, send_sem, recv_sem, device):
    return pltpu.make_async_remote_copy(
        src_ref=src,
        dst_ref=dst,
        send_sem=send_sem,
        recv_sem=recv_sem,
        device_id=device,
        device_id_type=MESH,
    )


def arrived(ref, sem):
    pltpu.make_async_copy(ref, ref, sem).wait()


def kernel(
    a_in, b_in, out,
    a_0, a_1, a_2, a_3, v_0, v_1, v_2, v_3, b_all, b_raw, b_wide, part, part16, sums16, total, total16, mirror16,
    b_sem, a_ready, swap_send, side_send, side_recv,
    an_send, an_recv, af_send, af_recv, as_send, as_recv,
    bn_send, bn_recv, bf_send, bf_recv,
    rs_send, rs_recv, t_send, t_recv,
):
    a_all, via = (a_0, a_1, a_2, a_3), (v_0, v_1, v_2, v_3)
    row, col, l = lax.axis_index("row"), lax.axis_index("col"), lax.axis_index("ka")
    z, h = row // 2, row % 2
    y, p = col // 2, col % 2
    x = 2 * h + l

    def dev(x, y, z, p):
        return (z * 2 + x // 2, y * 2 + p, x % 2)

    yp, ym, ya = (y + 1) % 4, (y + 3) % 4, (y + 2) % 4
    zp, zm, za = (z + 1) % 4, (z + 3) % 4, (z + 2) % 4
    y_next, y_prev = dev(x, yp, z, p), dev(x, ym, z, p)
    z_next, z_prev = dev(x, y, zp, p), dev(x, y, zm, p)
    sibling = dev(x, y, z, 1 - p)
    partner = dev((x + 2) % 4, y, z, 1 - p)
    x_others = [dev((x + d) % 4, y, z, p) for d in (1, 2, 3)]
    mirrors = [dev(2 * p + t, z, y, h) for t in (0, 1)]
    swaps = p != h
    on_self = jnp.logical_and(y == z, p == h)

    def j_of(jj):
        return ((jj % 2 + p + y) % 2) * 2 + jj // 2

    b_copy = pltpu.make_async_copy(b_in, b_raw, b_sem)
    b_copy.start()

    def a_part(u, half):
        return a_in.at[pl.ds(2 * half, 2), :, pl.ds(STARTS[u], SIZES[u]), :]

    @pl.when(jnp.logical_not(swaps))
    def _():
        for u in range(CHUNKS):
            for half in (0, 1):
                pltpu.make_async_copy(
                    a_part(u, half), a_all[u].at[p, y, pl.ds(2 * half, 2)], a_ready.at[u, half]
                ).start()

    barrier = pltpu.get_barrier_semaphore()

    def greet(device):
        pl.semaphore_signal(barrier, inc=1, device_id=device, device_id_type=MESH)

    for device in [y_next, y_prev, z_next, z_prev, sibling] + x_others:
        greet(device)

    @pl.when(swaps)
    def _():
        greet(partner)

    for t in (0, 1):
        @pl.when(jnp.logical_not(jnp.logical_and(on_self, l == t)))
        def _(t=t):
            greet(mirrors[t])

    def relayout(js):
        for j in js:
            jj = (j % 2) * 2 + (j // 2 + p + y) % 2
            for k in range(8):
                b_all[jj, z, k] = b_wide[k, pl.ds(j, 128, stride=4), :].astype(BF16)

    b_copy.wait()
    for k in range(8):
        b_wide[k] = b_raw[k].astype(F32)
    relayout((0, 2))

    peers = 9 + jnp.where(swaps, 1, 0) + jnp.where(on_self, 0, 1)
    pl.semaphore_wait(barrier, peers)

    def swap(u):
        return send(
            a_part(u, 0), a_all[u].at[1 - p, y, pl.ds(0, 2)], swap_send.at[u], a_ready.at[u, 0], partner
        )

    def swap_side(u):
        return send(a_part(u, 1), via[u], side_send.at[u], side_recv.at[u], sibling)

    def swap_on(u):
        return send(
            via[u], a_all[u].at[p, y, pl.ds(2, 2)], swap_send.at[u], a_ready.at[u, 1], x_others[1]
        )

    @pl.when(swaps)
    def _():
        for u in range(CHUNKS):
            swap_side(u).start()
            swap(u).start()

    def a_piece(u, place, half):
        return a_all[u].at[p, place, pl.ds(2 * half, 2)]

    def b_piece(u, place, half):
        return b_all.at[u, place, pl.ds(4 * half, 4)]

    def a_near(u, way, half):
        piece = a_piece(u, y, half)
        return send(piece, piece, an_send.at[u, way, half], an_recv.at[u, way, half], (y_next, y_prev)[way])

    def b_near(u, way, half):
        piece = b_piece(u, z, half)
        return send(piece, piece, bn_send.at[u, way, half], bn_recv.at[u, way, half], (z_next, z_prev)[way])

    def a_far(u, way):
        piece = a_piece(u, (ym, yp)[way], way)
        return send(piece, piece, af_send.at[u, way], af_recv.at[u, way], (y_next, y_prev)[way])

    def b_far(u, way):
        piece = b_piece(u, (zm, zp)[way], way)
        return send(piece, piece, bf_send.at[u, way], bf_recv.at[u, way], (z_next, z_prev)[way])

    def a_side(u, n):
        slot = a_all[u].at[p, (y, ym, yp, ya)[n]]
        return send(slot, slot, as_send.at[u, n], as_recv.at[u, n], sibling)

    def b_first(u):
        b_near(u, 0, 0).start()
        b_near(u, 1, 1).start()

    def b_second(u):
        b_near(u, 0, 1).start()
        b_near(u, 1, 0).start()

    def a_first(u):
        for half in (0, 1):
            arrived(a_piece(u, y, half), a_ready.at[u, half])
        a_near(u, 0, 0).start()
        a_near(u, 1, 1).start()

    def a_second(u):
        a_near(u, 0, 1).start()
        a_near(u, 1, 0).start()
        a_side(u, 0).start()

    def first(u):
        for way in (0, 1):
            arrived(b_piece(u, (zm, zp)[way], way), bn_recv.at[u, way, way])
            b_far(u, way).start()
        if u + 1 < CHUNKS:
            b_second(u + 1)
        for way in (0, 1):
            arrived(a_piece(u, (ym, yp)[way], way), an_recv.at[u, way, way])
            a_far(u, way).start()
        if u + 1 < CHUNKS:
            a_second(u + 1)

    def second(u):
        for way in (0, 1):
            arrived(b_piece(u, (zm, zp)[way], 1 - way), bn_recv.at[u, way, 1 - way])
        if u + 2 < CHUNKS:
            b_first(u + 2)
        for way in (0, 1):
            arrived(a_piece(u, (ym, yp)[way], 1 - way), an_recv.at[u, way, 1 - way])
            a_side(u, 1 + way).start()
        if u + 2 < CHUNKS:
            a_first(u + 2)

    def rs_copy(g, d):
        span = pl.ds(*GROUP_SPAN[g])
        there = (x + d) % 4
        return send(
            part16.at[there // 2, there % 2, span],
            sums16.at[d - 1, span],
            rs_send.at[g, d - 1],
            rs_recv.at[g, d - 1],
            x_others[d - 1],
        )

    def groups_of(t):
        return [g for g, (when, _) in enumerate(FLAT) if when == t]

    def product(u, jjs, places):
        total = None
        for s in places:
            left = jnp.concatenate(
                [a_all[u][:, s, :, k].reshape(8 * SIZES[u], 128) for k in range(8)], axis=1
            )
            right = jnp.concatenate([b_all[jj, s].reshape(1024, 128) for jj in jjs], axis=1)
            one = jnp.dot(left, right, preferred_element_type=F32)
            total = one if total is None else total + one
        return total

    def put(g, u, jjs, value, add):
        size = 2 * SIZES[u]
        tops = []
        for n, jj in enumerate(jjs):
            block = value[:, n * 128 : (n + 1) * 128]
            at = pl.ds(PLAIN[u, jj], size)
            if add:
                block = block + part[:, :, at].reshape(4 * size, 128)
            part[:, :, at] = block.reshape(2, 2, size, 128)
            tops.append(jnp.max(jnp.abs(block), axis=0, keepdims=True))
        return tops

    def send_group(g, tops):
        top = jnp.full((1, 128), 1e-30, F32)
        for one in tops:
            top = jnp.maximum(top, one)
        top16 = top.astype(BF16)
        top = top16.astype(F32)
        for u, jj in GROUP_BLOCKS[g]:
            size = 2 * SIZES[u]
            part16[:, :, pl.ds(GROUP_ROW[u, jj], size)] = encode(part[:, :, pl.ds(PLAIN[u, jj], size)], top)
        end = sum(GROUP_SPAN[g])
        part16[:, :, pl.ds(end - 16, 16)] = jnp.broadcast_to(top16, (2, 2, 16, 128))
        for d in (2, 1, 3):
            rs_copy(g, d).start()

    def side_arrived(t, n):
        arrived(a_all[t].at[1 - p, (y, ym, yp, ya)[n]], as_recv.at[t, n])

    def far(t):
        for way in (0, 1):
            arrived(a_piece(t, ya, way), af_recv.at[t, way])
        a_side(t, 3).start()
        for way in (0, 1):
            arrived(b_piece(t, za, way), bf_recv.at[t, way])

    def early(t):
        for n in range(3):
            side_arrived(t, n)
        for g in reversed(groups_of(t)):
            us, jjs = FLAT[g][1]
            if us == (t,) and t not in jjs:
                put(g, t, jjs, product(t, jjs, (y, ym, yp)), False)
            elif us != (t,):
                for u in us:
                    put(g, u, jjs, product(u, jjs, (z, zm, zp)), False)

    def late(t):
        far(t)
        side = True
        for g in reversed(groups_of(t)):
            us, jjs = FLAT[g][1]
            tops = []
            if us == (t,) and side:
                side_arrived(t, 3)
                side = False
            if us != (t,):
                for u in us:
                    tops += put(g, u, jjs, product(u, jjs, (za,)), True)
            else:
                if t in jjs:
                    tops += put(g, t, jjs, product(t, jjs, range(4)), False)
                else:
                    tops += put(g, t, jjs, product(t, jjs, (ya,)), True)
            send_group(g, tops)

    def run_span(r):
        return pl.ds(*RUN_SPAN[r])

    def mirror_remote(r):
        there = dev(2 * p + (RUNS[r][2] + p + y) % 2, z, y, h)
        return send(total16.at[run_span(r)], mirror16.at[l, run_span(r)], t_send.at[r], t_recv.at[r, l], there)

    def mirror_local(r):
        return pltpu.make_async_copy(total16.at[run_span(r)], mirror16.at[l, run_span(r)], t_recv.at[r, l])

    def mirror_here(r):
        return jnp.logical_and(on_self, (RUNS[r][2] + p + y) % 2 == l)

    def top_of(ref, end):
        return ref[pl.ds(end - 16, 16)].astype(F32)[:1]

    def reduce(t):
        for g in reversed(groups_of(t)):
            for d in (0, 2, 1):
                arrived(sums16.at[d, pl.ds(*GROUP_SPAN[g])], rs_recv.at[g, d])
            tops = [top_of(sums16.at[d], sum(GROUP_SPAN[g])) for d in range(3)]
            for r, (group, us, jj) in enumerate(RUNS):
                if group != g:
                    continue
                top = jnp.full((1, 128), 1e-30, F32)
                for u in us:
                    size = 2 * SIZES[u]
                    value = part[h, l, pl.ds(PLAIN[u, jj], size)]
                    for d in range(3):
                        value = value + decode(sums16[d, pl.ds(GROUP_ROW[u, jj], size)], tops[d])
                    total[pl.ds(PLAIN[u, jj], size)] = value
                    top = jnp.maximum(top, jnp.max(jnp.abs(value), axis=0, keepdims=True))
                    out[:, j_of(jj), pl.ds(STARTS[u], SIZES[u]), :] = value.reshape(2, SIZES[u], 128)
                top16 = top.astype(BF16)
                top = top16.astype(F32)
                for u in us:
                    size = 2 * SIZES[u]
                    total16[pl.ds(RUN_ROW[u, jj], size)] = encode(total[pl.ds(PLAIN[u, jj], size)], top)
                total16[pl.ds(sum(RUN_SPAN[r]) - 16, 16)] = jnp.broadcast_to(top16, (16, 128))

                @pl.when(mirror_here(r))
                def _(r=r):
                    mirror_local(r).start()

                @pl.when(jnp.logical_not(mirror_here(r)))
                def _(r=r):
                    mirror_remote(r).start()

    def sums_left(t):
        for g in groups_of(t):
            for d in (1, 2, 3):
                rs_copy(g, d).wait_send()

    def rings_left():
        for t in range(CHUNKS):
            for way in (0, 1):
                for half in (0, 1):
                    a_near(t, way, half).wait_send()
                    b_near(t, way, half).wait_send()
                a_far(t, way).wait_send()
                b_far(t, way).wait_send()
            for n in range(4):
                a_side(t, n).wait_send()

        @pl.when(swaps)
        def _():
            for u in range(CHUNKS):
                swap_side(u).wait_send()
                swap(u).wait_send()

        @pl.when(jnp.logical_not(swaps))
        def _():
            for u in range(CHUNKS):
                swap_on(u).wait_send()

    last = CHUNKS - 1
    b_first(0)
    b_second(0)
    b_first(1)

    @pl.when(jnp.logical_not(swaps))
    def _():
        a_first(0)
        a_second(0)
        a_first(1)
        for u in range(CHUNKS):
            arrived(via[u], side_recv.at[u])
            swap_on(u).start()

    relayout((1, 3))

    @pl.when(swaps)
    def _():
        a_first(0)
        a_second(0)
        a_first(1)

    for t in range(CHUNKS):
        first(t)
        second(t)
        early(t)
        if t >= 1:
            reduce(t - 1)
        late(t)
    rings_left()
    for t in range(last):
        sums_left(t)
    reduce(last)
    sums_left(last)

    for half in (0, 1):
        @pl.when((l + h + z) % 2 == half)
        def _(half=half):
            for r, (_, _, jj) in enumerate(RUNS):
                if jj % 2 == half:
                    for n in (0, 1):
                        arrived(mirror16.at[n, run_span(r)], t_recv.at[r, n])
            for i in (0, 1):
                jj = 2 * i + half
                for n in (0, 1):
                    pieces = []
                    for u in range(CHUNKS):
                        (r,) = [r for r, (_, us, at) in enumerate(RUNS) if u in us and at == jj]
                        top = top_of(mirror16.at[n], sum(RUN_SPAN[r]))
                        pieces.append(decode(mirror16[n, pl.ds(RUN_ROW[u, jj], 2 * SIZES[u])], top))
                    for m in (0, 1):
                        tile = jnp.concatenate(
                            [piece[m * SIZES[u] : (m + 1) * SIZES[u]] for u, piece in enumerate(pieces)], axis=0
                        )
                        out[i, 2 * n + m] = out[i, 2 * n + m] + tile.T

    for r in range(len(RUNS)):
        @pl.when(jnp.logical_not(mirror_here(r)))
        def _(r=r):
            mirror_remote(r).wait_send()


def per_device(amplitudes, integrals):
    rows = integrals.reshape(8, 512, 128)
    dma = pltpu.SemaphoreType.DMA
    n = CHUNKS
    return pl.pallas_call(
        kernel,
        out_shape=jax.ShapeDtypeStruct((2, 4, 128, 128), F32),
        in_specs=[pl.BlockSpec(memory_space=pltpu.HBM)] * 2,
        out_specs=pl.BlockSpec(memory_space=pltpu.VMEM),
        scratch_shapes=[
            *[pltpu.VMEM((2, 4, 4, 8, size, 128), BF16) for size in SIZES],
            *[pltpu.VMEM((2, 8, size, 128), BF16) for size in SIZES],
            pltpu.VMEM((4, 4, 8, 128, 128), BF16),
            pltpu.VMEM((8, 512, 128), BF16),
            pltpu.VMEM((8, 512, 128), F32),
            pltpu.VMEM((2, 2, PLAIN_ROWS, 128), F32),
            pltpu.VMEM((2, 2, GROUP_ROWS, 128), BF16),
            pltpu.VMEM((3, GROUP_ROWS, 128), BF16),
            pltpu.VMEM((PLAIN_ROWS, 128), F32),
            pltpu.VMEM((RUN_ROWS, 128), BF16),
            pltpu.VMEM((2, RUN_ROWS, 128), BF16),
            dma, dma((n, 2)), dma((n,)), dma((n,)), dma((n,)),
            dma((n, 2, 2)), dma((n, 2, 2)), dma((n, 2)), dma((n, 2)), dma((n, 4)), dma((n, 4)),
            dma((n, 2, 2)), dma((n, 2, 2)), dma((n, 2)), dma((n, 2)),
            dma((len(FLAT), 3)), dma((len(FLAT), 3)), dma((len(RUNS),)), dma((len(RUNS), 2)),
        ],
        compiler_params=pltpu.CompilerParams(
            collective_id=0, has_side_effects=True, vmem_limit_bytes=62 << 20
        ),
        cost_estimate=pl.CostEstimate(flops=4 << 30, bytes_accessed=3 << 20, transcendentals=0),
        name="cycle_contraction",
    )(amplitudes, rows)


def solution(mesh):
    return jax.shard_map(
        per_device,
        mesh=mesh,
        in_specs=(P(None, "ka", "row", "col"), P("ka", "row", None, "col")),
        out_specs=P("ka", None, "row", "col"),
        check_vma=False,
    )
```

```python
import jax
import jax.numpy as jnp
from jax import lax
from jax.experimental import pallas as pl
from jax.experimental.pallas import tpu as pltpu
from jax.sharding import PartitionSpec as P

MESH = pl.DeviceIdType.MESH
CHUNKS = 4
SIZES = (32, 48, 32, 16)
STARTS = tuple(sum(SIZES[:u]) for u in range(CHUNKS))
F32 = jnp.float32
BF16 = jnp.bfloat16


GROUPS = [
    [((t,), (jj, jj + 1)[: t + 1 - jj]) for jj in range(0, t + 1, 2)] + [(us, (t,)) for us in ([], [(0,)], [(0, 1)], [(2,), (1,), (0,)])[t]]
    for t in range(CHUNKS)
]
FLAT = [(t, group) for t in range(CHUNKS) for group in GROUPS[t]]
RUNS = [(g, us, jj) for g, (_, (us, jjs)) in enumerate(FLAT) for jj in jjs]


def layout(parts, pad):
    rows, spans, at = {}, [], 0
    for blocks in parts:
        first = at
        for u, jj in blocks:
            rows[u, jj] = at
            at += 2 * SIZES[u]
        spans.append((first, at - first + pad))
        at += pad
    return rows, spans, at


GROUP_BLOCKS = [[(u, jj) for jj in jjs for u in us] for _, (us, jjs) in FLAT]
RUN_BLOCKS = [[(u, jj) for u in us] for _, us, jj in RUNS]
PLAIN, _, PLAIN_ROWS = layout(GROUP_BLOCKS, 0)
GROUP_ROW, GROUP_SPAN, GROUP_ROWS = layout(GROUP_BLOCKS, 16)
RUN_ROW, RUN_SPAN, RUN_ROWS = layout(RUN_BLOCKS, 16)


def encode(values, top):
    w = jnp.abs(values) * (255.0 / 16 / top) + 1.0 / 16
    w2 = w * w
    w4 = w2 * w2
    w8 = w4 * w4
    code = w8 * w8 * w8 * (w4 * w2 * w)
    return jnp.where(values < 0, -code, code).astype(BF16)


def decode(codes, top):
    codes = codes.astype(F32)
    w = jnp.exp2(jnp.log2(jnp.abs(codes)) * (1.0 / 31))
    size = (w - 1.0 / 16) * (top * (16.0 / 255))
    return jnp.where(codes < 0, -size, size)


def send(src, dst, send_sem, recv_sem, device):
    return pltpu.make_async_remote_copy(
        src_ref=src,
        dst_ref=dst,
        send_sem=send_sem,
        recv_sem=recv_sem,
        device_id=device,
        device_id_type=MESH,
    )


def arrived(ref, sem):
    pltpu.make_async_copy(ref, ref, sem).wait()


def kernel(
    a_in, b_in, out,
    a_0, a_1, a_2, a_3, v_0, v_1, v_2, v_3, b_all, b_raw, b_wide, part, part16, sums16, total, total16, mirror16,
    b_sem, a_ready, swap_send, side_send, side_recv,
    an_send, an_recv, af_send, af_recv, as_send, as_recv,
    bn_send, bn_recv, bf_send, bf_recv,
    rs_send, rs_recv, t_send, t_recv,
):
    a_all, via = (a_0, a_1, a_2, a_3), (v_0, v_1, v_2, v_3)
    row, col, l = lax.axis_index("row"), lax.axis_index("col"), lax.axis_index("ka")
    z, h = row // 2, row % 2
    y, p = col // 2, col % 2
    x = 2 * h + l

    def dev(x, y, z, p):
        return (z * 2 + x // 2, y * 2 + p, x % 2)

    yp, ym, ya = (y + 1) % 4, (y + 3) % 4, (y + 2) % 4
    zp, zm, za = (z + 1) % 4, (z + 3) % 4, (z + 2) % 4
    y_next, y_prev = dev(x, yp, z, p), dev(x, ym, z, p)
    z_next, z_prev = dev(x, y, zp, p), dev(x, y, zm, p)
    sibling = dev(x, y, z, 1 - p)
    partner = dev((x + 2) % 4, y, z, 1 - p)
    x_others = [dev((x + d) % 4, y, z, p) for d in (1, 2, 3)]
    mirrors = [dev(2 * p + t, z, y, h) for t in (0, 1)]
    swaps = p != h
    on_self = jnp.logical_and(y == z, p == h)

    def j_of(jj):
        return ((jj % 2 + p + y) % 2) * 2 + jj // 2

    b_copy = pltpu.make_async_copy(b_in, b_raw, b_sem)
    b_copy.start()

    def a_part(u, half):
        return a_in.at[pl.ds(2 * half, 2), :, pl.ds(STARTS[u], SIZES[u]), :]

    @pl.when(jnp.logical_not(swaps))
    def _():
        for u in range(CHUNKS):
            for half in (0, 1):
                pltpu.make_async_copy(
                    a_part(u, half), a_all[u].at[p, y, pl.ds(2 * half, 2)], a_ready.at[u, half]
                ).start()

    barrier = pltpu.get_barrier_semaphore()

    def greet(device):
        pl.semaphore_signal(barrier, inc=1, device_id=device, device_id_type=MESH)

    for device in [y_next, y_prev, z_next, z_prev, sibling] + x_others:
        greet(device)

    @pl.when(swaps)
    def _():
        greet(partner)

    for t in (0, 1):
        @pl.when(jnp.logical_not(jnp.logical_and(on_self, l == t)))
        def _(t=t):
            greet(mirrors[t])

    def relayout(js):
        for j in js:
            jj = (j % 2) * 2 + (j // 2 + p + y) % 2
            for k in range(8):
                b_all[jj, z, k] = b_wide[k, pl.ds(j, 128, stride=4), :].astype(BF16)

    b_copy.wait()
    for k in range(8):
        b_wide[k, pl.ds(0, 512)] = b_raw[k].astype(F32)
    relayout((0, 2))

    peers = 9 + jnp.where(swaps, 1, 0) + jnp.where(on_self, 0, 1)
    pl.semaphore_wait(barrier, peers)

    def swap(u):
        return send(
            a_part(u, 0), a_all[u].at[1 - p, y, pl.ds(0, 2)], swap_send.at[u], a_ready.at[u, 0], partner
        )

    def swap_side(u):
        return send(a_part(u, 1), via[u], side_send.at[u], side_recv.at[u], sibling)

    def swap_on(u):
        return send(
            via[u], a_all[u].at[p, y, pl.ds(2, 2)], swap_send.at[u], a_ready.at[u, 1], x_others[1]
        )

    @pl.when(swaps)
    def _():
        for u in range(CHUNKS):
            swap_side(u).start()
            swap(u).start()

    def a_piece(u, place, half):
        return a_all[u].at[p, place, pl.ds(2 * half, 2)]

    def b_piece(u, place, half):
        return b_all.at[u, place, pl.ds(4 * half, 4)]

    def a_near(u, way, half):
        piece = a_piece(u, y, half)
        return send(piece, piece, an_send.at[u, way, half], an_recv.at[u, way, half], (y_next, y_prev)[way])

    def b_near(u, way, half):
        piece = b_piece(u, z, half)
        return send(piece, piece, bn_send.at[u, way, half], bn_recv.at[u, way, half], (z_next, z_prev)[way])

    def a_far(u, way):
        piece = a_piece(u, (ym, yp)[way], way)
        return send(piece, piece, af_send.at[u, way], af_recv.at[u, way], (y_next, y_prev)[way])

    def b_far(u, way):
        piece = b_piece(u, (zm, zp)[way], way)
        return send(piece, piece, bf_send.at[u, way], bf_recv.at[u, way], (z_next, z_prev)[way])

    def a_side(u, n):
        slot = a_all[u].at[p, (y, ym, yp, ya)[n]]
        return send(slot, slot, as_send.at[u, n], as_recv.at[u, n], sibling)

    def b_first(u):
        b_near(u, 0, 0).start()
        b_near(u, 1, 1).start()

    def b_second(u):
        b_near(u, 0, 1).start()
        b_near(u, 1, 0).start()

    def a_first(u):
        for half in (0, 1):
            arrived(a_piece(u, y, half), a_ready.at[u, half])
        a_near(u, 0, 0).start()
        a_near(u, 1, 1).start()

    def a_second(u):
        a_near(u, 0, 1).start()
        a_near(u, 1, 0).start()
        a_side(u, 0).start()

    def first(u):
        for way in (0, 1):
            arrived(b_piece(u, (zm, zp)[way], way), bn_recv.at[u, way, way])
            b_far(u, way).start()
        if u + 1 < CHUNKS:
            b_second(u + 1)
        for way in (0, 1):
            arrived(a_piece(u, (ym, yp)[way], way), an_recv.at[u, way, way])
            a_far(u, way).start()
        if u + 1 < CHUNKS:
            a_second(u + 1)

    def second(u):
        for way in (0, 1):
            arrived(b_piece(u, (zm, zp)[way], 1 - way), bn_recv.at[u, way, 1 - way])
        if u + 2 < CHUNKS:
            b_first(u + 2)
        for way in (0, 1):
            arrived(a_piece(u, (ym, yp)[way], 1 - way), an_recv.at[u, way, 1 - way])
            a_side(u, 1 + way).start()
        if u + 2 < CHUNKS:
            a_first(u + 2)

    def rs_copy(g, d):
        span = pl.ds(*GROUP_SPAN[g])
        there = (x + d) % 4
        return send(
            part16.at[there // 2, there % 2, span],
            sums16.at[d - 1, span],
            rs_send.at[g, d - 1],
            rs_recv.at[g, d - 1],
            x_others[d - 1],
        )

    def groups_of(t):
        return [g for g, (when, _) in enumerate(FLAT) if when == t]

    def product(u, jjs, places):
        total = None
        for s in places:
            left = jnp.concatenate(
                [a_all[u][:, s, :, k].reshape(8 * SIZES[u], 128) for k in range(8)], axis=1
            )
            right = jnp.concatenate([b_all[jj, s].reshape(1024, 128) for jj in jjs], axis=1)
            one = jnp.dot(left, right, preferred_element_type=F32)
            total = one if total is None else total + one
        return total

    def put(g, u, jjs, value, add):
        size = 2 * SIZES[u]
        tops = []
        for n, jj in enumerate(jjs):
            block = value[:, n * 128 : (n + 1) * 128]
            at = pl.ds(PLAIN[u, jj], size)
            if add:
                block = block + part[:, :, at].reshape(4 * size, 128)
            part[:, :, at] = block.reshape(2, 2, size, 128)
            tops.append(jnp.max(jnp.abs(block), axis=0, keepdims=True))
        return tops

    def send_group(g, tops):
        top = jnp.full((1, 128), 1e-30, F32)
        for one in tops:
            top = jnp.maximum(top, one)
        top16 = top.astype(BF16)
        top = top16.astype(F32)
        for u, jj in GROUP_BLOCKS[g]:
            size = 2 * SIZES[u]
            part16[:, :, pl.ds(GROUP_ROW[u, jj], size)] = encode(part[:, :, pl.ds(PLAIN[u, jj], size)], top)
        end = sum(GROUP_SPAN[g])
        part16[:, :, pl.ds(end - 16, 16)] = jnp.broadcast_to(top16, (2, 2, 16, 128))
        for d in (2, 1, 3):
            rs_copy(g, d).start()

    def side_arrived(t, n):
        arrived(a_all[t].at[1 - p, (y, ym, yp, ya)[n]], as_recv.at[t, n])

    def far(t):
        for way in (0, 1):
            arrived(a_piece(t, ya, way), af_recv.at[t, way])
        a_side(t, 3).start()
        for way in (0, 1):
            arrived(b_piece(t, za, way), bf_recv.at[t, way])

    def early(t):
        for n in range(3):
            side_arrived(t, n)
        for g in reversed(groups_of(t)):
            us, jjs = FLAT[g][1]
            if us == (t,) and t not in jjs:
                put(g, t, jjs, product(t, jjs, (y, ym, yp)), False)
            elif us != (t,):
                for u in us:
                    put(g, u, jjs, product(u, jjs, (z, zm, zp)), False)

    def late(t):
        far(t)
        side = True
        for g in reversed(groups_of(t)):
            us, jjs = FLAT[g][1]
            tops = []
            if us == (t,) and side:
                side_arrived(t, 3)
                side = False
            if us != (t,):
                for u in us:
                    tops += put(g, u, jjs, product(u, jjs, (za,)), True)
            else:
                if t in jjs:
                    tops += put(g, t, jjs, product(t, jjs, range(4)), False)
                else:
                    tops += put(g, t, jjs, product(t, jjs, (ya,)), True)
            send_group(g, tops)

    def run_span(r):
        return pl.ds(*RUN_SPAN[r])

    def mirror_remote(r):
        there = dev(2 * p + (RUNS[r][2] + p + y) % 2, z, y, h)
        return send(total16.at[run_span(r)], mirror16.at[l, run_span(r)], t_send.at[r], t_recv.at[r, l], there)

    def mirror_local(r):
        return pltpu.make_async_copy(total16.at[run_span(r)], mirror16.at[l, run_span(r)], t_recv.at[r, l])

    def mirror_here(r):
        return jnp.logical_and(on_self, (RUNS[r][2] + p + y) % 2 == l)

    def top_of(ref, end):
        return ref[pl.ds(end - 16, 16)].astype(F32)[:1]

    def reduce(t):
        for g in reversed(groups_of(t)):
            for d in (0, 2, 1):
                arrived(sums16.at[d, pl.ds(*GROUP_SPAN[g])], rs_recv.at[g, d])
            tops = [top_of(sums16.at[d], sum(GROUP_SPAN[g])) for d in range(3)]
            for r, (group, us, jj) in enumerate(RUNS):
                if group != g:
                    continue
                top = jnp.full((1, 128), 1e-30, F32)
                for u in us:
                    size = 2 * SIZES[u]
                    value = part[h, l, pl.ds(PLAIN[u, jj], size)]
                    for d in range(3):
                        value = value + decode(sums16[d, pl.ds(GROUP_ROW[u, jj], size)], tops[d])
                    total[pl.ds(PLAIN[u, jj], size)] = value
                    top = jnp.maximum(top, jnp.max(jnp.abs(value), axis=0, keepdims=True))
                    out[:, j_of(jj), pl.ds(STARTS[u], SIZES[u]), :] = value.reshape(2, SIZES[u], 128)
                top16 = top.astype(BF16)
                top = top16.astype(F32)
                for u in us:
                    size = 2 * SIZES[u]
                    total16[pl.ds(RUN_ROW[u, jj], size)] = encode(total[pl.ds(PLAIN[u, jj], size)], top)
                total16[pl.ds(sum(RUN_SPAN[r]) - 16, 16)] = jnp.broadcast_to(top16, (16, 128))

                @pl.when(mirror_here(r))
                def _(r=r):
                    mirror_local(r).start()

                @pl.when(jnp.logical_not(mirror_here(r)))
                def _(r=r):
                    mirror_remote(r).start()

    def sums_left(t):
        for g in groups_of(t):
            for d in (1, 2, 3):
                rs_copy(g, d).wait_send()

    def rings_left():
        for t in range(CHUNKS):
            for way in (0, 1):
                for half in (0, 1):
                    a_near(t, way, half).wait_send()
                    b_near(t, way, half).wait_send()
                a_far(t, way).wait_send()
                b_far(t, way).wait_send()
            for n in range(4):
                a_side(t, n).wait_send()

        @pl.when(swaps)
        def _():
            for u in range(CHUNKS):
                swap_side(u).wait_send()
                swap(u).wait_send()

        @pl.when(jnp.logical_not(swaps))
        def _():
            for u in range(CHUNKS):
                swap_on(u).wait_send()

    last = CHUNKS - 1
    b_first(0)
    b_second(0)
    b_first(1)

    @pl.when(jnp.logical_not(swaps))
    def _():
        a_first(0)
        a_second(0)
        a_first(1)
        for u in range(CHUNKS):
            arrived(via[u], side_recv.at[u])
            swap_on(u).start()

    relayout((1, 3))

    @pl.when(swaps)
    def _():
        a_first(0)
        a_second(0)
        a_first(1)

    for t in range(CHUNKS):
        first(t)
        second(t)
        early(t)
        if t >= 1:
            reduce(t - 1)
        late(t)
    rings_left()
    for t in range(last):
        sums_left(t)
    reduce(last)
    sums_left(last)

    for r in range(len(RUNS)):
        @pl.when(jnp.logical_not(mirror_here(r)))
        def _(r=r):
            mirror_remote(r).wait_send()

    for half in (0, 1):
        @pl.when((l + h + z) % 2 == half)
        def _(half=half):
            for i in (1, 0):
                jj = 2 * i + half
                for r, run in enumerate(RUNS):
                    if run[2] == jj:
                        for n in (0, 1):
                            arrived(mirror16.at[n, run_span(r)], t_recv.at[r, n])
                for n in (0, 1):
                    pieces = []
                    for u in range(CHUNKS):
                        (r,) = [r for r, (_, us, at) in enumerate(RUNS) if u in us and at == jj]
                        top = top_of(mirror16.at[n], sum(RUN_SPAN[r]))
                        pieces.append(decode(mirror16[n, pl.ds(RUN_ROW[u, jj], 2 * SIZES[u])], top))
                    for m in (0, 1):
                        tile = jnp.concatenate(
                            [piece[m * SIZES[u] : (m + 1) * SIZES[u]] for u, piece in enumerate(pieces)], axis=0
                        )
                        out[i, 2 * n + m] = out[i, 2 * n + m] + tile.T


def per_device(amplitudes, integrals):
    rows = integrals.reshape(8, 512, 128)
    dma = pltpu.SemaphoreType.DMA
    n = CHUNKS
    return pl.pallas_call(
        kernel,
        out_shape=jax.ShapeDtypeStruct((2, 4, 128, 128), F32),
        in_specs=[pl.BlockSpec(memory_space=pltpu.HBM)] * 2,
        out_specs=pl.BlockSpec(memory_space=pltpu.VMEM),
        scratch_shapes=[
            *[pltpu.VMEM((2, 4, 4, 8, size, 128), BF16) for size in SIZES],
            *[pltpu.VMEM((2, 8, size, 128), BF16) for size in SIZES],
            pltpu.VMEM((4, 4, 8, 128, 128), BF16),
            pltpu.VMEM((8, 512, 128), BF16),
            pltpu.VMEM((8, 520, 128), F32),
            pltpu.VMEM((2, 2, PLAIN_ROWS, 128), F32),
            pltpu.VMEM((2, 2, GROUP_ROWS, 128), BF16),
            pltpu.VMEM((3, GROUP_ROWS, 128), BF16),
            pltpu.VMEM((PLAIN_ROWS, 128), F32),
            pltpu.VMEM((RUN_ROWS, 128), BF16),
            pltpu.VMEM((2, RUN_ROWS, 128), BF16),
            dma, dma((n, 2)), dma((n,)), dma((n,)), dma((n,)),
            dma((n, 2, 2)), dma((n, 2, 2)), dma((n, 2)), dma((n, 2)), dma((n, 4)), dma((n, 4)),
            dma((n, 2, 2)), dma((n, 2, 2)), dma((n, 2)), dma((n, 2)),
            dma((len(FLAT), 3)), dma((len(FLAT), 3)), dma((len(RUNS),)), dma((len(RUNS), 2)),
        ],
        compiler_params=pltpu.CompilerParams(
            collective_id=0, has_side_effects=True, vmem_limit_bytes=62 << 20
        ),
        cost_estimate=pl.CostEstimate(flops=4 << 30, bytes_accessed=3 << 20, transcendentals=0),
        name="cycle_contraction",
    )(amplitudes, rows)


def solution(mesh):
    return jax.shard_map(
        per_device,
        mesh=mesh,
        in_specs=(P(None, "ka", "row", "col"), P("ka", "row", None, "col")),
        out_specs=P("ka", None, "row", "col"),
        check_vma=False,
    )
```

```python
import jax
import jax.numpy as jnp
from jax import lax
from jax.experimental import pallas as pl
from jax.experimental.pallas import tpu as pltpu
from jax.sharding import PartitionSpec as P

MESH = pl.DeviceIdType.MESH
CHUNKS = 4
SIZES = (32, 48, 32, 16)
STARTS = tuple(sum(SIZES[:u]) for u in range(CHUNKS))
F32 = jnp.float32
BF16 = jnp.bfloat16


GROUPS = [
    [((t,), (jj, jj + 1)[: t + 1 - jj]) for jj in range(0, t + 1, 2)] + [(us, (t,)) for us in ([], [(0,)], [(0, 1)], [(2,), (1,), (0,)])[t]]
    for t in range(CHUNKS)
]
FLAT = [(t, group) for t in range(CHUNKS) for group in GROUPS[t]]
RUNS = [(g, us, jj) for g, (_, (us, jjs)) in enumerate(FLAT) for jj in jjs]


def layout(parts, pad):
    rows, spans, at = {}, [], 0
    for blocks in parts:
        first = at
        for u, jj in blocks:
            rows[u, jj] = at
            at += 2 * SIZES[u]
        spans.append((first, at - first + pad))
        at += pad
    return rows, spans, at


GROUP_BLOCKS = [[(u, jj) for jj in jjs for u in us] for _, (us, jjs) in FLAT]
RUN_BLOCKS = [[(u, jj) for u in us] for _, us, jj in RUNS]
PLAIN, _, PLAIN_ROWS = layout(GROUP_BLOCKS, 0)
GROUP_ROW, GROUP_SPAN, GROUP_ROWS = layout(GROUP_BLOCKS, 16)
RUN_ROW, RUN_SPAN, RUN_ROWS = layout(RUN_BLOCKS, 16)


def encode(values, top):
    w = jnp.abs(values) * (255.0 / 16 / top) + 1.0 / 16
    w2 = w * w
    w4 = w2 * w2
    w8 = w4 * w4
    code = w8 * w8 * w8 * (w4 * w2 * w)
    return jnp.where(values < 0, -code, code).astype(BF16)


def decode(codes, top):
    codes = codes.astype(F32)
    w = jnp.exp2(jnp.log2(jnp.abs(codes)) * (1.0 / 31))
    size = (w - 1.0 / 16) * (top * (16.0 / 255))
    return jnp.where(codes < 0, -size, size)


def send(src, dst, send_sem, recv_sem, device):
    return pltpu.make_async_remote_copy(
        src_ref=src,
        dst_ref=dst,
        send_sem=send_sem,
        recv_sem=recv_sem,
        device_id=device,
        device_id_type=MESH,
    )


def arrived(ref, sem):
    pltpu.make_async_copy(ref, ref, sem).wait()


def kernel(
    a_in, b_in, out,
    a_0, a_1, a_2, a_3, v_0, v_1, v_2, v_3, b_all, b_raw, b_wide, part, part16, sums16, total, total16, mirror16,
    b_sem, a_ready, swap_send, side_send, side_recv,
    an_send, an_recv, af_send, af_recv, as_send, as_recv,
    bn_send, bn_recv, bf_send, bf_recv,
    rs_send, rs_recv, t_send, t_recv,
):
    a_all, via = (a_0, a_1, a_2, a_3), (v_0, v_1, v_2, v_3)
    row, col, l = lax.axis_index("row"), lax.axis_index("col"), lax.axis_index("ka")
    z, h = row // 2, row % 2
    y, p = col // 2, col % 2
    x = 2 * h + l

    def dev(x, y, z, p):
        return (z * 2 + x // 2, y * 2 + p, x % 2)

    yp, ym, ya = (y + 1) % 4, (y + 3) % 4, (y + 2) % 4
    zp, zm, za = (z + 1) % 4, (z + 3) % 4, (z + 2) % 4
    y_next, y_prev = dev(x, yp, z, p), dev(x, ym, z, p)
    z_next, z_prev = dev(x, y, zp, p), dev(x, y, zm, p)
    sibling = dev(x, y, z, 1 - p)
    partner = dev((x + 2) % 4, y, z, 1 - p)
    x_others = [dev((x + d) % 4, y, z, p) for d in (1, 2, 3)]
    mirrors = [dev(2 * p + t, z, y, h) for t in (0, 1)]
    swaps = p != h
    on_self = jnp.logical_and(y == z, p == h)

    def j_of(jj):
        return ((jj % 2 + p + y) % 2) * 2 + jj // 2

    b_copy = pltpu.make_async_copy(b_in, b_raw, b_sem)
    b_copy.start()

    def a_part(u, half):
        return a_in.at[pl.ds(2 * half, 2), :, pl.ds(STARTS[u], SIZES[u]), :]

    @pl.when(jnp.logical_not(swaps))
    def _():
        for u in range(CHUNKS):
            for half in (0, 1):
                pltpu.make_async_copy(
                    a_part(u, half), a_all[u].at[p, y, pl.ds(2 * half, 2)], a_ready.at[u, half]
                ).start()

    barrier = pltpu.get_barrier_semaphore()

    def greet(device):
        pl.semaphore_signal(barrier, inc=1, device_id=device, device_id_type=MESH)

    for device in [y_next, y_prev, z_next, z_prev, sibling] + x_others:
        greet(device)

    @pl.when(swaps)
    def _():
        greet(partner)

    for t in (0, 1):
        @pl.when(jnp.logical_not(jnp.logical_and(on_self, l == t)))
        def _(t=t):
            greet(mirrors[t])

    def relayout(js):
        for j in js:
            jj = (j % 2) * 2 + (j // 2 + p + y) % 2
            for k in range(8):
                b_all[jj, z, k] = b_wide[k, pl.ds(j, 128, stride=4), :].astype(BF16)

    b_copy.wait()
    for k in range(8):
        b_wide[k, pl.ds(0, 512)] = b_raw[k].astype(F32)
    relayout((0, 2))

    peers = 9 + jnp.where(swaps, 1, 0) + jnp.where(on_self, 0, 1)
    pl.semaphore_wait(barrier, peers)

    def swap(u):
        return send(
            a_part(u, 0), a_all[u].at[1 - p, y, pl.ds(0, 2)], swap_send.at[u], a_ready.at[u, 0], partner
        )

    def swap_side(u):
        return send(a_part(u, 1), via[u], side_send.at[u], side_recv.at[u], sibling)

    def swap_on(u):
        return send(
            via[u], a_all[u].at[p, y, pl.ds(2, 2)], swap_send.at[u], a_ready.at[u, 1], x_others[1]
        )

    @pl.when(swaps)
    def _():
        for u in range(CHUNKS):
            swap_side(u).start()
            swap(u).start()

    def a_piece(u, place, half):
        return a_all[u].at[p, place, pl.ds(2 * half, 2)]

    def b_piece(u, place, half):
        return b_all.at[u, place, pl.ds(4 * half, 4)]

    def a_near(u, way, half):
        piece = a_piece(u, y, half)
        return send(piece, piece, an_send.at[u, way, half], an_recv.at[u, way, half], (y_next, y_prev)[way])

    def b_near(u, way, half):
        piece = b_piece(u, z, half)
        return send(piece, piece, bn_send.at[u, way, half], bn_recv.at[u, way, half], (z_next, z_prev)[way])

    def a_far(u, way):
        piece = a_piece(u, (ym, yp)[way], way)
        return send(piece, piece, af_send.at[u, way], af_recv.at[u, way], (y_next, y_prev)[way])

    def b_far(u, way):
        piece = b_piece(u, (zm, zp)[way], way)
        return send(piece, piece, bf_send.at[u, way], bf_recv.at[u, way], (z_next, z_prev)[way])

    def a_side(u, n):
        slot = a_all[u].at[p, (y, ym, yp)[n]]
        return send(slot, slot, as_send.at[u, n], as_recv.at[u, n], sibling)

    def a_side_far(u, way):
        piece = a_piece(u, ya, way)
        return send(piece, piece, as_send.at[u, 3 + way], as_recv.at[u, 3 + way], sibling)

    def b_first(u):
        b_near(u, 0, 0).start()
        b_near(u, 1, 1).start()

    def b_second(u):
        b_near(u, 0, 1).start()
        b_near(u, 1, 0).start()

    def a_first(u):
        for half in (0, 1):
            arrived(a_piece(u, y, half), a_ready.at[u, half])
        a_near(u, 0, 0).start()
        a_near(u, 1, 1).start()

    def a_second(u):
        a_near(u, 0, 1).start()
        a_near(u, 1, 0).start()
        a_side(u, 0).start()

    def first(u):
        for way in (0, 1):
            arrived(b_piece(u, (zm, zp)[way], way), bn_recv.at[u, way, way])
            b_far(u, way).start()
        if u + 1 < CHUNKS:
            b_second(u + 1)
        for way in (0, 1):
            arrived(a_piece(u, (ym, yp)[way], way), an_recv.at[u, way, way])
            a_far(u, way).start()
        if u + 1 < CHUNKS:
            a_second(u + 1)

    def second(u):
        for way in (0, 1):
            arrived(b_piece(u, (zm, zp)[way], 1 - way), bn_recv.at[u, way, 1 - way])
        if u + 2 < CHUNKS:
            b_first(u + 2)
        for way in (0, 1):
            arrived(a_piece(u, (ym, yp)[way], 1 - way), an_recv.at[u, way, 1 - way])
            a_side(u, 1 + way).start()
        if u + 2 < CHUNKS:
            a_first(u + 2)

    def rs_copy(g, d):
        span = pl.ds(*GROUP_SPAN[g])
        there = (x + d) % 4
        return send(
            part16.at[there // 2, there % 2, span],
            sums16.at[d - 1, span],
            rs_send.at[g, d - 1],
            rs_recv.at[g, d - 1],
            x_others[d - 1],
        )

    def groups_of(t):
        return [g for g, (when, _) in enumerate(FLAT) if when == t]

    def product(u, jjs, places):
        total = None
        for s in places:
            left = jnp.concatenate(
                [a_all[u][:, s, :, k].reshape(8 * SIZES[u], 128) for k in range(8)], axis=1
            )
            right = jnp.concatenate([b_all[jj, s].reshape(1024, 128) for jj in jjs], axis=1)
            one = jnp.dot(left, right, preferred_element_type=F32)
            total = one if total is None else total + one
        return total

    def put(g, u, jjs, value, add):
        size = 2 * SIZES[u]
        tops = []
        for n, jj in enumerate(jjs):
            block = value[:, n * 128 : (n + 1) * 128]
            at = pl.ds(PLAIN[u, jj], size)
            if add:
                block = block + part[:, :, at].reshape(4 * size, 128)
            part[:, :, at] = block.reshape(2, 2, size, 128)
            tops.append(jnp.max(jnp.abs(block), axis=0, keepdims=True))
        return tops

    def send_group(g, tops):
        top = jnp.full((1, 128), 1e-30, F32)
        for one in tops:
            top = jnp.maximum(top, one)
        top16 = top.astype(BF16)
        top = top16.astype(F32)
        for u, jj in GROUP_BLOCKS[g]:
            size = 2 * SIZES[u]
            part16[:, :, pl.ds(GROUP_ROW[u, jj], size)] = encode(part[:, :, pl.ds(PLAIN[u, jj], size)], top)
        end = sum(GROUP_SPAN[g])
        part16[:, :, pl.ds(end - 16, 16)] = jnp.broadcast_to(top16, (2, 2, 16, 128))
        for d in (2, 1, 3):
            rs_copy(g, d).start()

    def side_arrived(t, n):
        if n < 3:
            arrived(a_all[t].at[1 - p, (y, ym, yp)[n]], as_recv.at[t, n])
            return
        for way in (0, 1):
            arrived(a_all[t].at[1 - p, ya, pl.ds(2 * way, 2)], as_recv.at[t, 3 + way])

    def far(t):
        for way in (0, 1):
            arrived(a_piece(t, ya, way), af_recv.at[t, way])
            a_side_far(t, way).start()
        for way in (0, 1):
            arrived(b_piece(t, za, way), bf_recv.at[t, way])

    def early(t):
        for n in range(3):
            side_arrived(t, n)
        for g in reversed(groups_of(t)):
            us, jjs = FLAT[g][1]
            if us == (t,) and t not in jjs:
                put(g, t, jjs, product(t, jjs, (y, ym, yp)), False)
            elif us != (t,):
                for u in us:
                    put(g, u, jjs, product(u, jjs, (z, zm, zp)), False)

    def late(t):
        far(t)
        side = True
        for g in reversed(groups_of(t)):
            us, jjs = FLAT[g][1]
            tops = []
            if us == (t,) and side:
                side_arrived(t, 3)
                side = False
            if us != (t,):
                for u in us:
                    tops += put(g, u, jjs, product(u, jjs, (za,)), True)
            else:
                if t in jjs:
                    tops += put(g, t, jjs, product(t, jjs, range(4)), False)
                else:
                    tops += put(g, t, jjs, product(t, jjs, (ya,)), True)
            send_group(g, tops)

    def run_span(r):
        return pl.ds(*RUN_SPAN[r])

    def mirror_remote(r):
        there = dev(2 * p + (RUNS[r][2] + p + y) % 2, z, y, h)
        return send(total16.at[run_span(r)], mirror16.at[l, run_span(r)], t_send.at[r], t_recv.at[r, l], there)

    def mirror_local(r):
        return pltpu.make_async_copy(total16.at[run_span(r)], mirror16.at[l, run_span(r)], t_recv.at[r, l])

    def mirror_here(r):
        return jnp.logical_and(on_self, (RUNS[r][2] + p + y) % 2 == l)

    def top_of(ref, end):
        return ref[pl.ds(end - 16, 16)].astype(F32)[:1]

    def reduce(t):
        for g in reversed(groups_of(t)):
            for d in (0, 2, 1):
                arrived(sums16.at[d, pl.ds(*GROUP_SPAN[g])], rs_recv.at[g, d])
            tops = [top_of(sums16.at[d], sum(GROUP_SPAN[g])) for d in range(3)]
            for r, (group, us, jj) in enumerate(RUNS):
                if group != g:
                    continue
                top = jnp.full((1, 128), 1e-30, F32)
                for u in us:
                    size = 2 * SIZES[u]
                    value = part[h, l, pl.ds(PLAIN[u, jj], size)]
                    for d in range(3):
                        value = value + decode(sums16[d, pl.ds(GROUP_ROW[u, jj], size)], tops[d])
                    total[pl.ds(PLAIN[u, jj], size)] = value
                    top = jnp.maximum(top, jnp.max(jnp.abs(value), axis=0, keepdims=True))
                    out[:, j_of(jj), pl.ds(STARTS[u], SIZES[u]), :] = value.reshape(2, SIZES[u], 128)
                top16 = top.astype(BF16)
                top = top16.astype(F32)
                for u in us:
                    size = 2 * SIZES[u]
                    total16[pl.ds(RUN_ROW[u, jj], size)] = encode(total[pl.ds(PLAIN[u, jj], size)], top)
                total16[pl.ds(sum(RUN_SPAN[r]) - 16, 16)] = jnp.broadcast_to(top16, (16, 128))

                @pl.when(mirror_here(r))
                def _(r=r):
                    mirror_local(r).start()

                @pl.when(jnp.logical_not(mirror_here(r)))
                def _(r=r):
                    mirror_remote(r).start()

    def sums_left(t):
        for g in groups_of(t):
            for d in (1, 2, 3):
                rs_copy(g, d).wait_send()

    def rings_left():
        for t in range(CHUNKS):
            for way in (0, 1):
                for half in (0, 1):
                    a_near(t, way, half).wait_send()
                    b_near(t, way, half).wait_send()
                a_far(t, way).wait_send()
                b_far(t, way).wait_send()
            for n in range(3):
                a_side(t, n).wait_send()
            for way in (0, 1):
                a_side_far(t, way).wait_send()

        @pl.when(swaps)
        def _():
            for u in range(CHUNKS):
                swap_side(u).wait_send()
                swap(u).wait_send()

        @pl.when(jnp.logical_not(swaps))
        def _():
            for u in range(CHUNKS):
                swap_on(u).wait_send()

    last = CHUNKS - 1
    b_first(0)
    b_second(0)
    b_first(1)

    @pl.when(jnp.logical_not(swaps))
    def _():
        a_first(0)
        a_second(0)
        a_first(1)
        for u in range(CHUNKS):
            arrived(via[u], side_recv.at[u])
            swap_on(u).start()

    relayout((1, 3))

    @pl.when(swaps)
    def _():
        a_first(0)
        a_second(0)
        a_first(1)

    for t in range(CHUNKS):
        first(t)
        second(t)
        early(t)
        if t >= 1:
            reduce(t - 1)
        late(t)
    rings_left()
    for t in range(last):
        sums_left(t)
    reduce(last)
    sums_left(last)

    for r in range(len(RUNS)):
        @pl.when(jnp.logical_not(mirror_here(r)))
        def _(r=r):
            mirror_remote(r).wait_send()

    for half in (0, 1):
        @pl.when((l + h + z) % 2 == half)
        def _(half=half):
            for i in (1, 0):
                jj = 2 * i + half
                for r, run in enumerate(RUNS):
                    if run[2] == jj:
                        for n in (0, 1):
                            arrived(mirror16.at[n, run_span(r)], t_recv.at[r, n])
                for n in (0, 1):
                    pieces = []
                    for u in range(CHUNKS):
                        (r,) = [r for r, (_, us, at) in enumerate(RUNS) if u in us and at == jj]
                        top = top_of(mirror16.at[n], sum(RUN_SPAN[r]))
                        pieces.append(decode(mirror16[n, pl.ds(RUN_ROW[u, jj], 2 * SIZES[u])], top))
                    for m in (0, 1):
                        tile = jnp.concatenate(
                            [piece[m * SIZES[u] : (m + 1) * SIZES[u]] for u, piece in enumerate(pieces)], axis=0
                        )
                        out[i, 2 * n + m] = out[i, 2 * n + m] + tile.T


def per_device(amplitudes, integrals):
    rows = integrals.reshape(8, 512, 128)
    dma = pltpu.SemaphoreType.DMA
    n = CHUNKS
    return pl.pallas_call(
        kernel,
        out_shape=jax.ShapeDtypeStruct((2, 4, 128, 128), F32),
        in_specs=[pl.BlockSpec(memory_space=pltpu.HBM)] * 2,
        out_specs=pl.BlockSpec(memory_space=pltpu.VMEM),
        scratch_shapes=[
            *[pltpu.VMEM((2, 4, 4, 8, size, 128), BF16) for size in SIZES],
            *[pltpu.VMEM((2, 8, size, 128), BF16) for size in SIZES],
            pltpu.VMEM((4, 4, 8, 128, 128), BF16),
            pltpu.VMEM((8, 512, 128), BF16),
            pltpu.VMEM((8, 520, 128), F32),
            pltpu.VMEM((2, 2, PLAIN_ROWS, 128), F32),
            pltpu.VMEM((2, 2, GROUP_ROWS, 128), BF16),
            pltpu.VMEM((3, GROUP_ROWS, 128), BF16),
            pltpu.VMEM((PLAIN_ROWS, 128), F32),
            pltpu.VMEM((RUN_ROWS, 128), BF16),
            pltpu.VMEM((2, RUN_ROWS, 128), BF16),
            dma, dma((n, 2)), dma((n,)), dma((n,)), dma((n,)),
            dma((n, 2, 2)), dma((n, 2, 2)), dma((n, 2)), dma((n, 2)), dma((n, 5)), dma((n, 5)),
            dma((n, 2, 2)), dma((n, 2, 2)), dma((n, 2)), dma((n, 2)),
            dma((len(FLAT), 3)), dma((len(FLAT), 3)), dma((len(RUNS),)), dma((len(RUNS), 2)),
        ],
        compiler_params=pltpu.CompilerParams(
            collective_id=0, has_side_effects=True, vmem_limit_bytes=62 << 20
        ),
        cost_estimate=pl.CostEstimate(flops=4 << 30, bytes_accessed=3 << 20, transcendentals=0),
        name="cycle_contraction",
    )(amplitudes, rows)


def solution(mesh):
    return jax.shard_map(
        per_device,
        mesh=mesh,
        in_specs=(P(None, "ka", "row", "col"), P("ka", "row", None, "col")),
        out_specs=P("ka", None, "row", "col"),
        check_vma=False,
    )
```
